256 devices in a mesh: ex: 32 (over x_hi, z, core), layer: 8 (over x_lo, y).
Axes of the slice: x: 4 (x_hi: 2, x_lo: 2; x = x_hi * 2 + x_lo), y: 4, z: 8, core: 2. Of those that a mesh axis runs over, the one named last changes fastest.
Arguments:
- train_grads: bfloat16 [16384, 8, 8192], P('ex', 'layer'), may hold values from -6 to 6
- query_grads: bfloat16 [1024, 8, 8192], P('ex', 'layer'), may hold values from -6 to 6
- left_factor: float32 [8, 64, 64], P('layer'), may hold values from -0.4 to 0.4
- right_factor: float32 [8, 128, 128], P('layer'), may hold values from -0.3 to 0.3
- query_order: int32 [1024], replicated, may hold values from 0 to 1023, each once
Outputs:
- scores: float32 [16384, 1024], P('ex', 'layer')
The draws below stay inside these ranges and needn't reach their ends.
Inputs may be any that keep to these rules, and one draw needn't show every extreme that they name: `query_order`: each query index appears exactly once.
All inputs are finite; a program needn't handle non-finite values.
Results may differ from the reference program's by a relative error of at most 0.0059.
Values may be sent and summed in bfloat16 or wider, within the bound.
A program may use at most 128 MiB of HBM per device.

```python
import jax
import jax.numpy as jnp
from jax import lax

FA = 64
FB = 128
K = 8192
LAYERS = 8
TRAIN = 16384
QUERIES = 1024


def block_levels(key, extent, pieces, least, largest):
    loudness = 1.0
    for dim, shards_of in pieces:
        steps = jax.random.uniform(jax.random.fold_in(jax.random.fold_in(key, 6), dim), (shards_of,), jnp.float32, least / len(pieces), largest / len(pieces))
        loudness = loudness * jnp.repeat(jnp.exp(steps), extent[dim] // shards_of).reshape((-1,) + (1,) * (len(extent) - 1 - dim))
    return loudness


def normal_values(stream_key, extent, width, most, split=(), kind=jnp.bfloat16):
    result = jax.random.normal(stream_key, extent, jnp.float32) * width
    if len(split) > 0:
        result = block_levels(stream_key, extent, split, -0.22, 0.18) * result
    return jnp.clip(result, min=-most, max=most).astype(kind)


def setup_inputs(seed: int = 0) -> dict:
    key_list = jax.random.split(jax.random.key(seed), 6)
    return {
        "train_grads": normal_values(key_list[0], (TRAIN, LAYERS, K), 1.0, 6.0, ((0, 32), (1, 8))),
        "query_grads": normal_values(key_list[1], (QUERIES, LAYERS, K), 1.0, 6.0, ((0, 32), (1, 8))),
        "left_factor": normal_values(key_list[2], (LAYERS, FA, FA), 0.0625, 0.4, ((0, 8),), jnp.float32),
        "right_factor": normal_values(key_list[3], (LAYERS, FB, FB), 0.0442, 0.3, ((0, 8),), jnp.float32),
        "query_order": jax.random.permutation(key_list[4], QUERIES).astype(jnp.int32),
    }


def condition(block, left, right):
    count = block.shape[0]
    left_mat = (jnp.eye(FA, dtype=jnp.float32) + left).astype(jnp.bfloat16)
    right_mat = (jnp.eye(FB, dtype=jnp.float32) + right).astype(jnp.bfloat16)
    flat = block.reshape(count * FA, FB)
    mid = jnp.dot(flat, right_mat, preferred_element_type=jnp.float32).astype(jnp.bfloat16)
    mid = mid.reshape(count, FA, FB)
    out = jnp.einsum('ab,qbc->qac', left_mat.astype(jnp.float32), mid.astype(jnp.float32))
    return out.reshape(count, FA * FB).astype(jnp.bfloat16)

def reference(train_grads, query_grads, left_factor, right_factor, query_order):
    partial_value = jnp.zeros((TRAIN, QUERIES), jnp.float32)
    for level in range(LAYERS):
        conditioned = condition(query_grads[:, level, :], left_factor[level], right_factor[level])
        partial_value = partial_value + lax.dot_general(train_grads[:, level, :], conditioned, (((1,), (1,)), ((), ())), preferred_element_type=jnp.float32)
    picked = jnp.take(partial_value, query_order.astype(jnp.int32), axis=1)
    return picked / jnp.sqrt(jnp.float32(K * LAYERS))
```

```python
import functools

import jax
import jax.numpy as jnp
from jax import lax
from jax.experimental import pallas as pl
from jax.experimental.pallas import tpu as pltpu
from jax.sharding import PartitionSpec as P

FA = 64
FB = 128
MESH = pl.DeviceIdType.MESH

Z = 8
GROUP = 8
SLOTS = 16
PART = 4
Q_PARTS = (0, 1)
P_PARTS = (2, 3)
FWD, BWD = 0, 1
LAST = 4
REACH = {0: (4, 3), 1: (3, 4), 2: (4, 3), 3: (3, 4)}


def slot_of(step, way, other):
    if step == 0:
        return other
    if step == LAST:
        return 14 + other
    return 2 + 4 * (step - 1) + 2 * other + way


BATCHES = ((0, 2), (2, 4), (6, 4), (10, 4), (14, 2))


def kernel(cond_ref, grads_ref, order_ref, out_ref, grads, block, acc, tile, pick, inbox, outbox, final,
           load_sem, main_recv, z_send, zb_send, x_send, sib_send, sib_recv, red_send, red_recv, fin_send, fin_recv):
    ex, me = lax.axis_index("ex"), lax.axis_index("layer")
    core = lax.rem(ex, 2)
    z = lax.rem(ex // 2, Z)
    hi = ex // (2 * Z)
    wide = block.shape[3] // PART

    def at(h, zz, c):
        return h * (2 * Z) + zz * 2 + c

    z_next = (at(hi, lax.rem(z + 1, Z), core), me)
    z_prev = (at(hi, lax.rem(z + Z - 1, Z), core), me)
    across = (at(1 - hi, z, core), me)
    sibling = (at(hi, z, 1 - core), me)
    peers = [(ex, lax.rem(me + j, GROUP)) for j in range(1, GROUP)]

    load = pltpu.make_async_copy(grads_ref, grads, load_sem)
    load.start()

    barrier = pltpu.get_barrier_semaphore()
    partners = [z_next, z_prev, across, sibling] + peers
    for d in partners:
        pl.semaphore_signal(barrier, inc=1, device_id=d, device_id_type=MESH)

    block[0, core] = cond_ref[...]
    for s in range(SLOTS):
        step = 0 if s < 2 else LAST if s >= 14 else 1 + (s - 2) // 4
        other = s % 2 if s < 2 or s >= 14 else ((s - 2) // 2) % 2
        way = 0 if s < 2 or s >= 14 else (s - 2) % 2
        zz = lax.rem(z + (Z - step if way == FWD else step), Z)
        hh = 1 - hi if other else hi
        first = (hh * Z + zz) * 64
        ids = first + lax.broadcasted_iota(jnp.int32, (64, pick.shape[1]), 0)
        pick[s * 64:(s + 1) * 64, :] = jnp.where(ids == order_ref[...], 1.0, 0.0).astype(jnp.bfloat16)

    pl.semaphore_wait(barrier, len(partners))

    def chunk(s, c, k):
        return block.at[s, c, :, pl.ds(k * wide, wide)]

    sent = []

    def send(s, to, k, device, send_sem, recv_sem):
        copy = pltpu.make_async_remote_copy(
            src_ref=chunk(s, core, k), dst_ref=chunk(to, core, k), send_sem=send_sem, recv_sem=recv_sem,
            device_id=device, device_id_type=MESH)
        copy.start()
        sent.append(copy)

    def send_z(step, way, other, k):
        s, to = slot_of(step, way, other), slot_of(step + 1, way, other)
        if way == FWD:
            send(s, to, k, z_next, z_send.at[s, k], main_recv.at[to, k])
        else:
            send(s, to, k, z_prev, zb_send.at[s, k] if step == 0 else z_send.at[s, k], main_recv.at[to, k])

    def send_x(step, way, k):
        s, to = slot_of(step, way, 0), slot_of(step, way, 1)
        send(s, to, k, across, x_send.at[s, k], main_recv.at[to, k])

    def send_sib(s, k):
        send(s, s, k, sibling, sib_send.at[s, k], sib_recv.at[s, k])

    def wait_main(s, k):
        pltpu.make_async_remote_copy(
            src_ref=chunk(s, core, k), dst_ref=chunk(s, core, k), send_sem=z_send.at[s, k],
            recv_sem=main_recv.at[s, k], device_id=sibling, device_id_type=MESH).wait_recv()

    def wait_sib(s, k):
        pltpu.make_async_remote_copy(
            src_ref=chunk(s, 1 - core, k), dst_ref=chunk(s, 1 - core, k), send_sem=sib_send.at[s, k],
            recv_sem=sib_recv.at[s, k], device_id=sibling, device_id_type=MESH).wait_recv()

    def compute(b):
        first, count = BATCHES[b]
        for s in range(first, first + count):
            for k in range(PART):
                wait_sib(s, k)
        if b == 0:
            load.wait()
        w = count * 64
        acc[:, :w] = jnp.zeros((acc.shape[0], w), jnp.float32)

        @pl.loop(0, PART)
        def _(i):
            cols = pl.ds(pl.multiple_of(i * wide, wide), wide)
            rhs = block[first:first + count, :, :, cols].reshape(w, wide)
            acc[:, :w] += lax.dot_general(grads[:, cols], rhs, (((1,), (1,)), ((), ())),
                                          preferred_element_type=jnp.float32)

        at_cols = slice(first * 64, first * 64 + w)
        tile[:, at_cols] = acc[:, :w].astype(jnp.bfloat16)
        for j, peer in enumerate(peers):
            rows = pl.ds(pl.multiple_of(peer[1] * 64, 64), 64)
            copy = pltpu.make_async_remote_copy(
                src_ref=tile.at[rows, at_cols], dst_ref=inbox.at[j, :, at_cols],
                send_sem=red_send.at[b, j], recv_sem=red_recv.at[b, j], device_id=peer, device_id_type=MESH)
            copy.start()
            reduces.append(copy)

    reduces = []

    for k in P_PARTS:
        send_x(0, 0, k)
    for k in range(PART):
        send_z(0, FWD, 0, k)
        send_z(0, BWD, 0, k)
    for k in range(PART):
        send_sib(0, k)
    for k in P_PARTS:
        wait_main(1, k)
        send_z(0, FWD, 1, k)
        send_z(0, BWD, 1, k)
        send_sib(1, k)
    for k in Q_PARTS:
        send_x(0, 0, k)

    for step in range(1, LAST + 1):
        for k, other in ((0, 0), (1, 0), (2, 0), (3, 0), (2, 1), (3, 1)):
            for way in (FWD, BWD):
                if REACH[k][way] < step:
                    continue
                s = slot_of(step, way, other)
                wait_main(s, k)
                if REACH[k][way] > step:
                    send_z(step, way, other, k)
                if k in Q_PARTS:
                    send_x(step, way, k)
                send_sib(s, k)
            if k == 1:
                for w in (FWD, BWD) if step > 1 else (FWD,):
                    for q in Q_PARTS:
                        s = slot_of(step - 1, w, 1)
                        wait_main(s, q)
                        send_sib(s, q)
                compute(step - 1)
    for q in Q_PARTS:
        s = slot_of(LAST, 0, 1)
        wait_main(s, q)
        send_sib(s, q)
    compute(LAST)

    for copy in reduces:
        copy.wait_recv()
    total = tile[pl.ds(pl.multiple_of(me * 64, 64), 64), :].astype(jnp.float32)
    for j in range(GROUP - 1):
        total += inbox[j].astype(jnp.float32)
    total = total * (1.0 / 256.0)
    high = total.astype(jnp.bfloat16)
    low = (total - high.astype(jnp.float32)).astype(jnp.bfloat16)
    scores = jnp.dot(high, pick[...], preferred_element_type=jnp.float32)
    scores += jnp.dot(low, pick[...], preferred_element_type=jnp.float32)
    for m in range(GROUP):
        outbox[m] = scores[:, m * 128:(m + 1) * 128]
    finals = []
    for j, peer in enumerate(peers):
        copy = pltpu.make_async_remote_copy(
            src_ref=outbox.at[peer[1]], dst_ref=final.at[me], send_sem=fin_send.at[j], recv_sem=fin_recv.at[j],
            device_id=peer, device_id_type=MESH)
        copy.start()
        finals.append(copy)
    final[me] = outbox[me]
    for copy in sent:
        copy.wait_send()
    for copy in reduces:
        copy.wait_send()
    for copy in finals:
        copy.wait()
    out_ref[...] = final[...].reshape(out_ref.shape)


def condition(block, left, right):
    count = block.shape[0]
    left_mat = (jnp.eye(FA, dtype=jnp.float32) + left).astype(jnp.bfloat16)
    right_mat = (jnp.eye(FB, dtype=jnp.float32) + right).astype(jnp.bfloat16)
    flat = block.reshape(count * FA, FB)
    mid = jnp.dot(flat, right_mat, preferred_element_type=jnp.float32).astype(jnp.bfloat16)
    mid = mid.reshape(count, FA, FB)
    out = jnp.einsum("ab,qbc->qac", left_mat, mid, preferred_element_type=jnp.float32)
    return out.reshape(count, FA * FB).astype(jnp.bfloat16)


def local(train_grads, query_grads, left_factor, right_factor, query_order):
    grads = train_grads[:, 0, :]
    outgoing = condition(query_grads[:, 0, :], left_factor[0], right_factor[0])
    rows, depth = grads.shape
    own = outgoing.shape[0]
    queries = query_order.shape[0]
    dma = pltpu.SemaphoreType.DMA
    return pl.pallas_call(
        kernel,
        name="scores",
        out_shape=jax.ShapeDtypeStruct((rows, queries // GROUP), jnp.float32),
        in_specs=[
            pl.BlockSpec(memory_space=pltpu.VMEM),
            pl.BlockSpec(memory_space=pl.ANY),
            pl.BlockSpec(memory_space=pltpu.VMEM),
        ],
        out_specs=pl.BlockSpec(memory_space=pltpu.VMEM),
        scratch_shapes=[
            pltpu.VMEM((rows, depth), jnp.bfloat16),
            pltpu.VMEM((SLOTS, 2, own, depth), jnp.bfloat16),
            pltpu.VMEM((rows, 256), jnp.float32),
            pltpu.VMEM((rows, queries), jnp.bfloat16),
            pltpu.VMEM((queries, queries), jnp.bfloat16),
            pltpu.VMEM((GROUP - 1, rows // GROUP, queries), jnp.bfloat16),
            pltpu.VMEM((GROUP, rows // GROUP, queries // GROUP), jnp.float32),
            pltpu.VMEM((GROUP, rows // GROUP, queries // GROUP), jnp.float32),
            dma,
            dma((SLOTS, PART)),
            dma((SLOTS, PART)),
            dma((2, PART)),
            dma((SLOTS, PART)),
            dma((SLOTS, PART)),
            dma((SLOTS, PART)),
            dma((len(BATCHES), GROUP - 1)),
            dma((len(BATCHES), GROUP - 1)),
            dma((GROUP - 1,)),
            dma((GROUP - 1,)),
        ],
        compiler_params=pltpu.CompilerParams(
            collective_id=0, has_side_effects=True, vmem_limit_bytes=48 * 2**20
        ),
        cost_estimate=pl.CostEstimate(
            flops=2 * rows * depth * queries, bytes_accessed=rows * depth * 2, transcendentals=0
        ),
    )(outgoing, grads, query_order.reshape(1, queries))


def solution(mesh):
    return jax.shard_map(
        local,
        mesh=mesh,
        in_specs=(
            P("ex", "layer", None),
            P("ex", "layer", None),
            P("layer", None, None),
            P("layer", None, None),
            P(),
        ),
        out_specs=P("ex", "layer"),
        check_vma=False,
    )
```

```python
import functools

import jax
import jax.numpy as jnp
from jax import lax
from jax.experimental import pallas as pl
from jax.experimental.pallas import tpu as pltpu
from jax.sharding import PartitionSpec as P

FA = 64
FB = 128
MESH = pl.DeviceIdType.MESH

Z = 8
GROUP = 8
FWD, BWD = 0, 1
LAST = 4

NEAR, WIDE = 0, 1
QUARTERS = 4

SLOTS = 16
FIRST = 14

ARRIVALS = 34
OWN_NEAR, OWN_WIDE, THEIR_WIDE, THEIR_NEAR = range(4)


def slot_of(step, way, other):
    return 2 + 4 * (step - 1) + 2 * other + way


def arrival(step, way, what):
    return 2 + 8 * (step - 1) + 4 * way + what


def eye_plus(mat):
    n = mat.shape[0]
    rows = lax.broadcasted_iota(jnp.int32, (n, n), 0)
    cols = lax.broadcasted_iota(jnp.int32, (n, n), 1)
    return (jnp.where(rows == cols, 1.0, 0.0) + mat).astype(jnp.bfloat16)


def condition(raw, left, right, by_row, by_query, out):
    count = raw.shape[0]
    left_mat, right_mat = eye_plus(left[...]), eye_plus(right[...])
    group = 16
    for a in range(0, FA, group):
        rows = jnp.concatenate([raw[:, i * FB:(i + 1) * FB] for i in range(a, a + group)], axis=0)
        mid = jnp.dot(rows, right_mat, preferred_element_type=jnp.float32).astype(jnp.bfloat16).astype(jnp.float32)
        for i in range(group):
            by_query[pl.ds(a + i, count, stride=FA), :] = mid[i * count:(i + 1) * count, :]
    group = 8
    for q in range(0, count, group):
        mid = jnp.concatenate([by_query[i * FA:(i + 1) * FA, :] for i in range(q, q + group)], axis=1)
        done = jnp.dot(left_mat, mid.astype(jnp.bfloat16), preferred_element_type=jnp.float32)
        for i in range(group):
            by_row[pl.ds(q + i, FA, stride=count), :] = done[:, i * FB:(i + 1) * FB]
    for a in range(FA):
        out[:, a * FB:(a + 1) * FB] = by_row[a * count:(a + 1) * count, :].astype(jnp.bfloat16)


def kernel(raw_ref, grads_ref, left_ref, right_ref, order_ref, out_ref, raw, left, right, order, by_row, by_query,
           grads, block, acc, tile, pick, scores, inbox, outbox, final,
           load_sem, main_recv, z_send, x_send, sib_send, sib_recv, red_send, red_recv, fin_send, fin_recv):
    ex, me = lax.axis_index("ex"), lax.axis_index("layer")
    core = lax.rem(ex, 2)
    z = lax.rem(ex // 2, Z)
    hi = ex // (2 * Z)
    depth = block.shape[3]
    half, quarter = depth // 2, depth // QUARTERS

    def at(h, zz, c):
        return h * (2 * Z) + zz * 2 + c

    z_next = (at(hi, lax.rem(z + 1, Z), core), me)
    z_prev = (at(hi, lax.rem(z + Z - 1, Z), core), me)
    toward = (z_next, z_prev)
    across = (at(1 - hi, z, core), me)
    sibling = (at(hi, z, 1 - core), me)

    def peer_of(j):
        return ex, lax.rem(me + j + 1, GROUP)

    loads = [pltpu.make_async_copy(src, dst, load_sem.at[i]) for i, (src, dst) in enumerate(
        ((raw_ref, raw), (right_ref, right), (left_ref, left), (order_ref, order), (grads_ref, grads)))]
    for load in loads[:4]:
        load.start()

    barrier = pltpu.get_barrier_semaphore()
    for d in (z_next, z_prev, across, sibling):
        pl.semaphore_signal(barrier, inc=1, device_id=d, device_id_type=MESH)

    @pl.loop(0, GROUP - 1)
    def _(j):
        pl.semaphore_signal(barrier, inc=1, device_id=peer_of(j), device_id_type=MESH)

    for load in loads[:3]:
        load.wait()
    condition(raw, left, right, by_row, by_query, block.at[0, core])
    loads[4].start()
    pl.semaphore_wait(barrier, 4 + GROUP - 1)

    def part(s, c, start, width):
        return block.at[s, c, :, pl.ds(start, width)]

    def remote(src, dst, send_sem, recv_sem, device):
        return pltpu.make_async_remote_copy(src_ref=src, dst_ref=dst, send_sem=send_sem, recv_sem=recv_sem,
                                            device_id=device, device_id_type=MESH)

    def send_z(step, way, s, to, start, width, signal):
        remote(part(s, core, start, width), part(to, core, start, width), z_send.at[step], main_recv.at[signal],
               toward[way]).start()

    def send_x(step, s, to, start, width, signal):
        remote(part(s, core, start, width), part(to, core, start, width), x_send.at[step], main_recv.at[signal],
               across).start()

    def send_sib(batch, s, start, width):
        remote(part(s, core, start, width), part(s, core, start, width), sib_send.at[batch], sib_recv.at[batch],
               sibling).start()

    def arrived(s, start, width, signal):
        here = part(s, core, start, width)
        remote(here, here, z_send.at[0], main_recv.at[signal], sibling).wait_recv()

    def sib_batch(batch, first, count, start, width):
        here = block.at[pl.ds(first, count), 1 - core, :, pl.ds(start, width)]
        return remote(here, here, sib_send.at[batch], sib_recv.at[batch], sibling)

    def multiply(first, count, k):
        w = count * 64
        cols = pl.ds(pl.multiple_of(k * quarter, quarter), quarter)
        rhs = block[pl.ds(first, count), :, :, cols].reshape(w, quarter)
        acc[:, :w] += lax.dot_general(grads[:, cols], rhs, (((1,), (1,)), ((), ())),
                                      preferred_element_type=jnp.float32)

    def clear():
        acc[...] = jnp.zeros_like(acc)

    def pass_on(b, start, width, kind):
        tile[:, pl.ds(start, width)] = acc[:, :width].astype(jnp.bfloat16)

        @pl.loop(0, GROUP - 1)
        def _(j):
            peer = peer_of(j)
            rows, cols = pl.ds(pl.multiple_of(peer[1] * 64, 64), 64), pl.ds(start, width)
            remote(tile.at[rows, cols], inbox.at[j, :, cols], red_send.at[b], red_recv.at[kind], peer).start()

    def reduced(b, kind, start, width):
        here = inbox.at[:, :, pl.ds(start, width)]
        return remote(here, here, red_send.at[b], red_recv.at[kind], sibling)

    def batch(b):
        first = slot_of(b, 0, 0)
        sib_batch(b, first, 4, 0, depth).wait_recv()
        clear()

        @pl.loop(0, QUARTERS)
        def _(k):
            multiply(first, 4, k)
        start = 128 + 256 * (b - 1)
        pass_on(b, start if isinstance(b, int) else pl.multiple_of(start, 128), 256, 0)

    send_x(0, 0, 1, half, half, 0)
    for what, start in ((OWN_NEAR, 0), (OWN_WIDE, half)):
        for way in (FWD, BWD):
            send_z(0, way, 0, slot_of(1, way, 0), start, half, arrival(1, way, what))
    send_sib(0, 0, 0, depth)
    clear()
    loads[3].wait()

    @pl.loop(0, SLOTS)
    def _(i):
        edge = (i < 2) | (i >= FIRST)
        step = (i + 2) // 4
        other = jnp.where(edge, lax.rem(i, 2), lax.rem((i + 2) // 2, 2))
        back = jnp.where(edge, 0, lax.rem(i, 2))
        zz = lax.rem(z + jnp.where(back == 1, step, Z - step), Z)
        hh = jnp.where(other == 1, 1 - hi, hi)
        ids = (hh * Z + zz) * 64 + lax.broadcasted_iota(jnp.int32, (64, pick.shape[1]), 0)
        pick[pl.ds(pl.multiple_of(i * 64, 64), 64), :] = jnp.where(ids == order[...], 1.0, 0.0).astype(jnp.bfloat16)

    arrived(1, half, half, 0)
    for way in (FWD, BWD):
        send_z(0, way, 1, slot_of(1, way, 1), half, half, arrival(1, way, THEIR_WIDE))
    send_sib(0, 1, half, half)
    send_x(0, 0, 1, 0, half, 1)
    loads[4].wait()

    @pl.loop(1, LAST)
    def _(step):
        def arrive(what, other, start):
            for way in (FWD, BWD):
                s = slot_of(step, way, other)
                arrived(s, start, half, arrival(step, way, what))

                @pl.when(step < LAST - 1)
                def _():
                    send_z(step, way, s, slot_of(step + 1, way, other), start, half, arrival(step + 1, way, what))

                @pl.when(step == LAST - 1)
                def _():
                    k = start // quarter + way
                    send_z(step, way, s, FIRST + other, k * quarter, quarter, 26 + 4 * other + k)

                if what == OWN_NEAR:
                    send_x(step, s, slot_of(step, way, 1), start, half, arrival(step, way, THEIR_NEAR))
                send_sib(step, s, start, half)

        arrive(OWN_NEAR, 0, 0)

        @pl.when(step == 1)
        def _():
            arrived(1, 0, half, 1)
            send_sib(0, 1, 0, half)
            sib_batch(0, 0, 2, 0, depth).wait_recv()

            @pl.loop(0, QUARTERS)
            def _(k):
                multiply(0, 2, k)
            pass_on(0, 0, 128, 0)

        @pl.when(step > 1)
        def _():
            for way in (FWD, BWD):
                s = slot_of(step - 1, way, 1)
                arrived(s, 0, half, arrival(step - 1, way, THEIR_NEAR))
                send_sib(step - 1, s, 0, half)
            batch(step - 1)

        arrive(OWN_WIDE, 0, half)
        arrive(THEIR_WIDE, 1, half)

    for k in (0, 1):
        arrived(FIRST, k * quarter, quarter, 26 + k)
        send_x(LAST, FIRST, FIRST + 1, k * quarter, quarter, 30 + k)
        send_sib(LAST + k, FIRST, k * quarter, quarter)
    for way in (FWD, BWD):
        s = slot_of(LAST - 1, way, 1)
        arrived(s, 0, half, arrival(LAST - 1, way, THEIR_NEAR))
        send_sib(LAST - 1, s, 0, half)
    batch(LAST - 1)
    clear()
    for k in (2, 3):
        arrived(FIRST, k * quarter, quarter, 26 + k)
        send_sib(LAST + k, FIRST, k * quarter, quarter)
    for k in (0, 1):
        arrived(FIRST + 1, k * quarter, quarter, 30 + k)
        send_sib(LAST + k, FIRST + 1, k * quarter, quarter)

    @pl.loop(0, 2)
    def _(k):
        sib_batch(LAST + k, FIRST, 2, pl.multiple_of(k * quarter, quarter), quarter).wait_recv()
        multiply(FIRST, 2, k)
    for k in (2, 3):
        arrived(FIRST + 1, k * quarter, quarter, 30 + k)
        send_sib(LAST + k, FIRST + 1, k * quarter, quarter)

    mine = pl.ds(pl.multiple_of(me * 64, 64), 64)

    def ordered(start, width):
        total = tile[mine, start:start + width].astype(jnp.float32)
        for j in range(GROUP - 1):
            total += inbox[j, :, start:start + width].astype(jnp.float32)
        total = total * (1.0 / 256.0)
        high = total.astype(jnp.bfloat16)
        low = (total - high.astype(jnp.float32)).astype(jnp.bfloat16)
        both = jnp.dot(jnp.concatenate([high, low], axis=0), pick[start:start + width, :],
                       preferred_element_type=jnp.float32)
        return both[:64] + both[64:]

    early = FIRST * 64
    reduced(0, 0, 0, early).wait_recv()
    scores[...] = ordered(0, early)

    @pl.loop(2, QUARTERS)
    def _(k):
        sib_batch(LAST + k, FIRST, 2, pl.multiple_of(k * quarter, quarter), quarter).wait_recv()
        multiply(FIRST, 2, k)
    pass_on(LAST, early, 128, 1)
    reduced(LAST, 1, early, 128).wait_recv()
    done = (scores[...] + ordered(early, 128)).astype(jnp.bfloat16)
    for m in range(GROUP):
        outbox[m] = done[:, m * 128:(m + 1) * 128]

    @pl.loop(0, GROUP - 1)
    def _(j):
        peer = peer_of(j)
        remote(outbox.at[peer[1]], final.at[me], fin_send.at[0], fin_recv.at[0], peer).start()
    final[me] = outbox[me]

    for step in range(LAST):
        here = block.at[0:3, core, :, 0:depth if step < LAST - 1 else half]
        remote(here, here, z_send.at[step], main_recv.at[0], sibling).wait_send()
    for step in range(LAST + 1):
        here = block.at[0:2, core, :, 0:half] if step < LAST else block.at[0:1, core, :, 0:half]
        remote(here, here, x_send.at[step], main_recv.at[0], sibling).wait_send()
    for b in range(LAST):
        sib_batch(b, 0, 4 if b else 2, 0, depth).wait_send()
    for k in range(QUARTERS):
        sib_batch(LAST + k, 0, 2, 0, quarter).wait_send()
    for b in range(LAST + 1):
        reduced(b, 0, 0, 256 if 0 < b < LAST else 128).wait_send()
    all_but_one = final.at[0:GROUP - 1]
    whole = remote(all_but_one, all_but_one, fin_send.at[0], fin_recv.at[0], sibling)
    whole.wait_send()
    whole.wait_recv()
    out_ref[...] = final[...].reshape(out_ref.shape).astype(jnp.float32)


def local(train_grads, query_grads, left_factor, right_factor, query_order):
    grads = train_grads[:, 0, :]
    raw = query_grads[:, 0, :]
    rows, depth = grads.shape
    own = raw.shape[0]
    queries = query_order.shape[0]
    dma = pltpu.SemaphoreType.DMA
    return pl.pallas_call(
        kernel,
        name="scores",
        out_shape=jax.ShapeDtypeStruct((rows, queries // GROUP), jnp.float32),
        in_specs=[pl.BlockSpec(memory_space=pl.ANY)] * 5,
        out_specs=pl.BlockSpec(memory_space=pltpu.VMEM),
        scratch_shapes=[
            pltpu.VMEM((own, depth), jnp.bfloat16),
            pltpu.VMEM((FA, FA), jnp.float32),
            pltpu.VMEM((FB, FB), jnp.float32),
            pltpu.VMEM((1, queries), jnp.int32),
            pltpu.VMEM((own * FA, FB), jnp.float32),
            pltpu.VMEM((own * FA, FB), jnp.float32),
            pltpu.VMEM((rows, depth), jnp.bfloat16),
            pltpu.VMEM((SLOTS, 2, own, depth), jnp.bfloat16),
            pltpu.VMEM((rows, 256), jnp.float32),
            pltpu.VMEM((rows, queries), jnp.bfloat16),
            pltpu.VMEM((queries, queries), jnp.bfloat16),
            pltpu.VMEM((rows // GROUP, queries), jnp.float32),
            pltpu.VMEM((GROUP - 1, rows // GROUP, queries), jnp.bfloat16),
            pltpu.VMEM((GROUP, rows // GROUP, queries // GROUP), jnp.bfloat16),
            pltpu.VMEM((GROUP, rows // GROUP, queries // GROUP), jnp.bfloat16),
            dma((5,)),
            dma((ARRIVALS,)),
            dma((LAST,)),
            dma((LAST + 1,)),
            dma((LAST + QUARTERS,)),
            dma((LAST + QUARTERS,)),
            dma((LAST + 1,)),
            dma((2,)),
            dma((1,)),
            dma((1,)),
        ],
        compiler_params=pltpu.CompilerParams(
            collective_id=0, has_side_effects=True, vmem_limit_bytes=60 * 2**20
        ),
        cost_estimate=pl.CostEstimate(
            flops=2 * rows * depth * queries, bytes_accessed=rows * depth * 2, transcendentals=0
        ),
    )(raw, grads, left_factor[0], right_factor[0], query_order.reshape(1, queries))


def solution(mesh):
    return jax.shard_map(
        local,
        mesh=mesh,
        in_specs=(
            P("ex", "layer", None),
            P("ex", "layer", None),
            P("layer", None, None),
            P("layer", None, None),
            P(),
        ),
        out_specs=P("ex", "layer"),
        check_vma=False,
    )
```

```python
import functools

import jax
import jax.numpy as jnp
from jax import lax
from jax.experimental import pallas as pl
from jax.experimental.pallas import tpu as pltpu
from jax.sharding import PartitionSpec as P

FA = 64
FB = 128
MESH = pl.DeviceIdType.MESH

Z = 8
GROUP = 8
FWD, BWD = 0, 1
WAYS = (FWD, BWD)

PIECES = (
    ("N", 0, 0), ("W", 0, 0), ("TW", 0, 0), ("TN", 0, 0), ("N", 1, 0), ("N", 1, 1), ("W", 1, 0), ("W", 1, 1),
    ("N", 2, 0), ("N", 2, 1), ("TW", 1, 0), ("TW", 1, 1), ("TN", 1, 0), ("TN", 1, 1), ("N", 3, 0), ("N", 3, 1),
    ("W", 2, 0), ("W", 2, 1), ("TN", 2, 0), ("TN", 2, 1), ("N", 4, 0), ("TW", 2, 0), ("TW", 2, 1), None,
    ("TN", 3, 0), ("TN", 3, 1), ("W", 3, 0), ("W", 3, 1), ("TN", 4, 0), None, None, None,
    ("TW", 3, 0), ("TW", 3, 1), ("W", 4, 0), ("TW", 4, 0),
)
BATCHES = ((0, 8), (8, 8), (16, 7), (24, 5), (32, 4))
FINAL = 35
NEAR_SUMS = 3
COLUMNS = 32 * len(PIECES)


def place(kind, step, way):
    return PIECES.index((kind, step, way if 0 < step < 4 else 0))


def batch_of(piece):
    return len(BATCHES) if piece == FINAL else piece // 8


SECOND = {place("N", 4, 0): 36, place("W", 4, 0): 37, place("TN", 4, 0): 38, FINAL: 39}
ARRIVALS = 42


def eye_plus(mat):
    n = mat.shape[0]
    rows = lax.broadcasted_iota(jnp.int32, (n, n), 0)
    cols = lax.broadcasted_iota(jnp.int32, (n, n), 1)
    return (jnp.where(rows == cols, 1.0, 0.0) + mat).astype(jnp.bfloat16)


def condition(raw, left_mat, right_mat, by_row, by_query, out):
    count = raw.shape[0]
    group = 16
    for a in range(0, FA, group):
        rows = jnp.concatenate([raw[:, i * FB:(i + 1) * FB] for i in range(a, a + group)], axis=0)
        mid = jnp.dot(rows, right_mat, preferred_element_type=jnp.float32).astype(jnp.bfloat16).astype(jnp.float32)
        for i in range(group):
            by_query[pl.ds(a + i, count, stride=FA), :] = mid[i * count:(i + 1) * count, :]
    group = 8
    for q in range(0, count, group):
        mid = jnp.concatenate([by_query[i * FA:(i + 1) * FA, :] for i in range(q, q + group)], axis=1)
        done = jnp.dot(left_mat, mid.astype(jnp.bfloat16), preferred_element_type=jnp.float32)
        for i in range(group):
            by_row[pl.ds(q + i, FA, stride=count), :] = done[:, i * FB:(i + 1) * FB]
    for a in range(FA):
        out[:, a * FB:(a + 1) * FB] = by_row[a * count:(a + 1) * count, :].astype(jnp.bfloat16)


def kernel(raw_ref, grads_ref, left_ref, right_ref, order_ref, out_ref, raw, left, right, order, by_row, by_query,
           grads, block, acc, tile, pick, scores, sums, halves, inbox, inbox_y, inbox_x, outbox, final,
           load_sem, main_recv, z_send, x_send, sib_send, sib_recv, red_send, red_recv, swap_send, swap_recv, fin_send, fin_recv):
    ex, me = lax.axis_index("ex"), lax.axis_index("layer")
    core = lax.rem(ex, 2)
    z = lax.rem(ex // 2, Z)
    hi = ex // (2 * Z)
    depth = block.shape[3]
    half, quarter = depth // 2, depth // 4

    def at(h, zz, c):
        return h * (2 * Z) + zz * 2 + c

    toward = ((at(hi, lax.rem(z + 1, Z), core), me), (at(hi, lax.rem(z + Z - 1, Z), core), me))
    across = (at(1 - hi, z, core), me)
    sibling = (at(hi, z, 1 - core), me)

    y, lo = lax.rem(me, 4), me // 4
    aside = (ex, lax.rem(me + 4, GROUP))

    def peer_of(j):
        return ex, lax.rem(me + j + 1, GROUP)

    def along_y(j):
        return ex, lo * 4 + lax.rem(y + j + 1, 4)

    def rows_of(device):
        return 2 * lax.rem(device[1], 4) + device[1] // 4

    loads = [pltpu.make_async_copy(src, dst, load_sem.at[i]) for i, (src, dst) in enumerate(
        ((raw_ref, raw), (right_ref, right), (left_ref, left), (order_ref, order), (grads_ref, grads)))]
    for load in loads[:4]:
        load.start()

    barrier = pltpu.get_barrier_semaphore()
    for d in (*toward, across, sibling):
        pl.semaphore_signal(barrier, inc=1, device_id=d, device_id_type=MESH)

    @pl.loop(0, GROUP - 1)
    def _(j):
        pl.semaphore_signal(barrier, inc=1, device_id=peer_of(j), device_id_type=MESH)

    for load in loads[:3]:
        load.wait()
    mats = eye_plus(left[...]), eye_plus(right[...])
    condition(raw.at[0:16], *mats, by_row, by_query, block.at[0, core])

    def remote(src, dst, send_sem, recv_sem, device):
        return pltpu.make_async_remote_copy(src_ref=src, dst_ref=dst, send_sem=send_sem, recv_sem=recv_sem,
                                            device_id=device, device_id_type=MESH)

    def part(piece, c, start, width):
        if width == depth:
            return block.at[piece, c]
        return block.at[piece, c, :, pl.ds(start if isinstance(start, int) else pl.multiple_of(start, width), width)]

    def send(src, dst, start, width, send_sem, signal, device):
        remote(part(src, core, start, width), part(dst, core, start, width), send_sem, main_recv.at[signal], device).start()

    def arrived(piece, start, width, signal):
        here = part(piece, core, start, width)
        remote(here, here, z_send.at[0], main_recv.at[signal], sibling).wait_recv()

    def send_sib(piece, start, width, group):
        here = part(piece, core, start, width)
        remote(here, here, sib_send.at[group], sib_recv.at[group], sibling).start()

    def round_z(kind, step, way):
        src, dst = place(kind, step, way), place(kind, step + 1, way)
        if step < 3:
            send(src, dst, 0, depth, z_send.at[step], dst, toward[way])
        elif dst != FINAL:
            send(src, dst, way * half, half, z_send.at[step], SECOND[dst] if way else dst, toward[way])
        else:
            for k in (2 * way, 2 * way + 1):
                send(src, dst, k * quarter, quarter, z_send.at[step], SECOND[dst] + k - 1 if k else dst, toward[way])

    def over_x(kind, step, way):
        src, dst = place(kind, step, way), place("T" + kind, step, way)
        if step < 4:
            send(src, dst, 0, depth, x_send.at[0], dst, across)
        else:
            send(src, dst, way * half, half, x_send.at[1], SECOND[dst] if way else dst, across)

    def take(kind, step, way):
        piece = place(kind, step, way)
        if step < 4:
            arrived(piece, 0, depth, piece)
            send_sib(piece, 0, depth, batch_of(piece))
        else:
            arrived(piece, way * half, half, SECOND[piece] if way else piece)
            send_sib(piece, way * half, half, batch_of(piece))

    def sib_batch(b):
        first, count = BATCHES[b]
        count -= b == len(BATCHES) - 1
        here = block.at[first:first + count, 1 - core]
        return remote(here, here, sib_send.at[b], sib_recv.at[b], sibling)

    def sib_last(k):
        here = part(FINAL, 1 - core, k * quarter, quarter)
        sem = len(BATCHES) + k
        return remote(here, here, sib_send.at[sem], sib_recv.at[sem], sibling)

    def product(first, count, start, width):
        cols = pl.ds(start if isinstance(start, int) else pl.multiple_of(start, width), width)
        rhs = block[first:first + count, :, :, cols].reshape(count * 32, width)
        return lax.dot_general(grads[:, cols], rhs, (((1,), (1,)), ((), ())), preferred_element_type=jnp.float32)

    def columns(b):
        first, count = BATCHES[b]
        return first * 32, 128 if count < 4 else 256

    def batch(b):
        first, count = BATCHES[b]
        sib_batch(b).wait_recv()
        w = count * 32
        acc[...] = jnp.zeros_like(acc)

        @pl.loop(0, 4)
        def _(i):
            k = i // 2 + 2 * lax.rem(i, 2)
            if b == len(BATCHES) - 1:
                sib_last(k).wait_recv()
            acc[:, :w] += product(first, count, k * quarter, quarter)
        start, width = columns(b)
        tile[:, start:start + w] = acc[:, :w].astype(jnp.bfloat16)

        cols = slice(start, start + width)
        if b >= NEAR_SUMS:
            to = slice(start - NEAR_SUMS * 256, start - NEAR_SUMS * 256 + width)

            @pl.loop(0, GROUP - 1)
            def _(j):
                peer = peer_of(j)
                rows = pl.ds(pl.multiple_of(rows_of(peer) * 64, 64), 64)
                remote(tile.at[rows, cols], inbox.at[j, :, to], red_send.at[b], red_recv.at[b], peer).start()
        else:
            @pl.loop(0, 3)
            def _(j):
                peer = along_y(j)
                rows = pl.ds(pl.multiple_of(lax.rem(peer[1], 4) * 128, 128), 128)
                remote(tile.at[rows, cols], inbox_y.at[j, :, cols], red_send.at[b], red_recv.at[b], peer).start()

    def reduced(b):
        start, width = columns(b)
        late = start - NEAR_SUMS * 256
        here = inbox.at[:, :, late:late + width] if b >= NEAR_SUMS else inbox_y.at[:, :, start:start + width]
        return remote(here, here, red_send.at[b], red_recv.at[b], sibling)

    def swap_x(b):
        start, width = columns(b)
        cols = slice(start, start + width)
        reduced(b).wait_recv()
        total = tile[pl.ds(pl.multiple_of(y * 128, 128), 128), cols].astype(jnp.float32)
        for j in range(3):
            total += inbox_y[j, :, cols].astype(jnp.float32)
        for i in range(2):
            sums[i, :, cols] = total[i * 64:(i + 1) * 64]
            halves[i, :, cols] = total[i * 64:(i + 1) * 64].astype(jnp.bfloat16)
        remote(halves.at[1 - lo, :, cols], inbox_x.at[:, cols], swap_send.at[b], swap_recv.at[0], aside).start()

    def swapped(start, width, b):
        here = inbox_x.at[:, start:start + width]
        return remote(here, here, swap_send.at[b], swap_recv.at[0], sibling)

    pl.semaphore_wait(barrier, 4 + GROUP - 1)
    for way in WAYS:
        round_z("N", 0, way)
    condition(raw.at[16:32], *mats, by_row, by_query, block.at[1, core])
    over_x("W", 0, 0)
    for way in WAYS:
        round_z("W", 0, way)
    for piece in (0, 1):
        send_sib(piece, 0, depth, 0)
    loads[4].start()

    loads[3].wait()
    row = lax.broadcasted_iota(jnp.int32, (32, 1), 0)
    row = row + 16 * (row // 16)

    def first_query(piece):
        kind, step, way = PIECES[piece]
        zz = lax.rem(z + (Z - step if way == FWD else step), Z)
        hh = 1 - hi if kind[0] == "T" else hi
        return (hh * Z + zz) * 64 + (16 if kind[-1] == "W" else 0)

    for piece in range(len(PIECES)):
        rows = slice(piece * 32, (piece + 1) * 32)
        if PIECES[piece] is None:
            pick[rows, :] = jnp.zeros((32, pick.shape[1]), jnp.bfloat16)
        else:
            pick[rows, :] = jnp.where(row + first_query(piece) == order[...], 1.0, 0.0).astype(jnp.bfloat16)
    tile[...] = jnp.zeros_like(tile)
    def ordered(total, start):
        high = total.astype(jnp.bfloat16)
        low = (total - high.astype(jnp.float32)).astype(jnp.bfloat16)
        both = jnp.dot(jnp.concatenate([high, low], axis=0), pick[start:start + total.shape[1], :],
                       preferred_element_type=jnp.float32)
        return both[:64] + both[64:]

    def late_sum(b):
        start, width = columns(b)
        reduced(b).wait_recv()
        total = tile[pl.ds(pl.multiple_of(rows_of((ex, me)) * 64, 64), 64), start:start + width].astype(jnp.float32)
        for j in range(GROUP - 1):
            total += inbox[j, :, start - NEAR_SUMS * 256:start - NEAR_SUMS * 256 + width].astype(jnp.float32)
        return ordered(total, start)

    for way in WAYS:
        take("N", 1, way)
        round_z("N", 1, way)
    over_x("N", 0, 0)
    for way in WAYS:
        over_x("N", 1, way)
    take("TW", 0, 0)
    for way in WAYS:
        round_z("TW", 0, way)
    for way in WAYS:
        take("W", 1, way)
    take("TN", 0, 0)
    loads[4].wait()
    batch(0)
    for way in WAYS:
        take("N", 2, way)
        round_z("N", 2, way)
        over_x("N", 2, way)
    for way in WAYS:
        round_z("W", 1, way)
    for kind in ("TW", "TN"):
        for way in WAYS:
            take(kind, 1, way)
    for way in WAYS:
        take("N", 3, way)
        round_z("N", 3, way)
        over_x("N", 3, way)
    for way in WAYS:
        round_z("TW", 1, way)
    swap_x(0)
    batch(1)
    for way in WAYS:
        take("W", 2, way)
        round_z("W", 2, way)
    for way in WAYS:
        take("N", 4, way)
        over_x("N", 4, way)
    for way in WAYS:
        take("TN", 2, way)
    for way in WAYS:
        take("TW", 2, way)
        round_z("TW", 2, way)
    swap_x(1)
    batch(2)
    for way in WAYS:
        take("W", 3, way)
        round_z("W", 3, way)
    for way in WAYS:
        take("TN", 3, way)
    for way in WAYS:
        take("TW", 3, way)
        round_z("TW", 3, way)
    for way in WAYS:
        take("TN", 4, way)
    swap_x(2)
    batch(3)
    for way in WAYS:
        take("W", 4, way)
    for k in (0, 2, 1, 3):
        arrived(FINAL, k * quarter, quarter, SECOND[FINAL] + k - 1 if k else FINAL)
        send_sib(FINAL, k * quarter, quarter, len(BATCHES) + k)
    batch(4)
    swapped(0, NEAR_SUMS * 256, 0).wait_recv()
    scores[...] = ordered(sums[lo] + inbox_x[...].astype(jnp.float32), 0)
    scores[...] += late_sum(3)
    done = (scores[...] + late_sum(4)).astype(jnp.bfloat16)
    for m in range(GROUP):
        outbox[m] = done[:, m * 128:(m + 1) * 128]

    @pl.loop(0, GROUP - 1)
    def _(j):
        peer = peer_of(j)
        remote(outbox.at[peer[1]], final.at[rows_of((ex, me))], fin_send.at[0], fin_recv.at[0], peer).start()
    final[rows_of((ex, me))] = outbox[me]

    def units(n, width, sem):
        here = block.at[0:n, core, :, 0:width]
        remote(here, here, sem, main_recv.at[0], sibling).wait_send()

    for step in range(4):
        units(6, depth if step < 3 else half, z_send.at[step])
    units(8, depth, x_send.at[0])
    units(2, half, x_send.at[1])
    for b in range(len(BATCHES)):
        sib_batch(b).wait_send()
        reduced(b).wait_send()
    for b in range(NEAR_SUMS):
        swapped(0, 256, b).wait_send()
    for k in range(4):
        sib_last(k).wait_send()
    whole = remote(final.at[0:GROUP - 1], final.at[0:GROUP - 1], fin_send.at[0], fin_recv.at[0], sibling)
    whole.wait_send()
    whole.wait_recv()
    out_ref[...] = final[...].reshape(out_ref.shape).astype(jnp.float32) * (1.0 / 256.0)


def local(train_grads, query_grads, left_factor, right_factor, query_order):
    grads = train_grads[:, 0, :]
    raw = query_grads[:, 0, :]
    rows, depth = grads.shape
    own = raw.shape[0]
    queries = query_order.shape[0]
    dma = pltpu.SemaphoreType.DMA
    return pl.pallas_call(
        kernel,
        name="scores",
        out_shape=jax.ShapeDtypeStruct((rows, queries // GROUP), jnp.float32),
        in_specs=[pl.BlockSpec(memory_space=pl.ANY)] * 5,
        out_specs=pl.BlockSpec(memory_space=pltpu.VMEM),
        scratch_shapes=[
            pltpu.VMEM((own, depth), jnp.bfloat16),
            pltpu.VMEM((FA, FA), jnp.float32),
            pltpu.VMEM((FB, FB), jnp.float32),
            pltpu.VMEM((1, queries), jnp.int32),
            pltpu.VMEM((own * FA, FB), jnp.float32),
            pltpu.VMEM((own * FA, FB), jnp.float32),
            pltpu.VMEM((rows, depth), jnp.bfloat16),
            pltpu.VMEM((len(PIECES), 2, own // 2, depth), jnp.bfloat16),
            pltpu.VMEM((rows, 256), jnp.float32),
            pltpu.VMEM((rows, COLUMNS), jnp.bfloat16),
            pltpu.VMEM((COLUMNS, queries), jnp.bfloat16),
            pltpu.VMEM((rows // GROUP, queries), jnp.float32),
            pltpu.VMEM((2, rows // GROUP, NEAR_SUMS * 256), jnp.float32),
            pltpu.VMEM((2, rows // GROUP, NEAR_SUMS * 256), jnp.bfloat16),
            pltpu.VMEM((GROUP - 1, rows // GROUP, COLUMNS - NEAR_SUMS * 256), jnp.bfloat16),
            pltpu.VMEM((3, rows // 4, NEAR_SUMS * 256), jnp.bfloat16),
            pltpu.VMEM((rows // GROUP, NEAR_SUMS * 256), jnp.bfloat16),
            pltpu.VMEM((GROUP, rows // GROUP, queries // GROUP), jnp.bfloat16),
            pltpu.VMEM((GROUP, rows // GROUP, queries // GROUP), jnp.bfloat16),
            dma((5,)),
            dma((ARRIVALS,)),
            dma((4,)),
            dma((2,)),
            dma((len(BATCHES) + 4,)),
            dma((len(BATCHES) + 4,)),
            dma((len(BATCHES),)),
            dma((len(BATCHES),)),
            dma((NEAR_SUMS,)),
            dma((1,)),
            dma((1,)),
            dma((1,)),
        ],
        compiler_params=pltpu.CompilerParams(
            collective_id=0, has_side_effects=True, vmem_limit_bytes=52 * 2**20
        ),
        cost_estimate=pl.CostEstimate(
            flops=2 * rows * depth * queries, bytes_accessed=rows * depth * 2, transcendentals=0
        ),
    )(*(pltpu.with_memory_space_constraint(x, pltpu.HBM) for x in (
        raw, grads, left_factor[0], right_factor[0], query_order.reshape(1, queries))))


def solution(mesh):
    return jax.shard_map(
        local,
        mesh=mesh,
        in_specs=(
            P("ex", "layer", None),
            P("ex", "layer", None),
            P("layer", None, None),
            P("layer", None, None),
            P(),
        ),
        out_specs=P("ex", "layer"),
        check_vma=False,
    )
```

```python
import functools

import jax
import jax.numpy as jnp
from jax import lax
from jax.experimental import pallas as pl
from jax.experimental.pallas import tpu as pltpu
from jax.sharding import PartitionSpec as P

FA = 64
FB = 128
MESH = pl.DeviceIdType.MESH

Z = 8
GROUP = 8
FWD, BWD = 0, 1
WAYS = (FWD, BWD)

PIECES = (
    ("N", 0, 0), ("W", 0, 0), ("TW", 0, 0), ("TN", 0, 0), ("N", 1, 0), ("N", 1, 1), ("W", 1, 0), ("W", 1, 1),
    ("N", 2, 0), ("N", 2, 1), ("TW", 1, 0), ("TW", 1, 1), ("TN", 1, 0), ("TN", 1, 1), ("N", 3, 0), ("N", 3, 1),
    ("W", 2, 0), ("W", 2, 1), ("TN", 2, 0), ("TN", 2, 1), ("N", 4, 0), ("TW", 2, 0), ("TW", 2, 1), ("W", 3, 0),
    ("TN", 3, 0), ("TN", 3, 1), ("W", 3, 1), ("TW", 3, 0), ("TW", 3, 1), ("TN", 4, 0), ("W", 4, 0), ("TW", 4, 0),
)
BATCHES = ((0, 8), (8, 8), (16, 8), (24, 8))
FINAL = 31
NEAR_SUMS = 3
COLUMNS = 32 * len(PIECES)


def place(kind, step, way):
    return PIECES.index((kind, step, way if 0 < step < 4 else 0))


def batch_of(piece):
    return len(BATCHES) if piece == FINAL else piece // 8


STRIP = 768

SECOND = {place("N", 4, 0): 32, place("W", 4, 0): 33, place("TN", 4, 0): 34, FINAL: 35}
STRIPS = {}
for kind in ("W", "TW"):
    for step in range(kind == "W", 5):
        for way in WAYS if step else (FWD,):
            STRIPS[kind, step, way] = 42 + len(STRIPS)
ARRIVALS = 42 + len(STRIPS)


def eye_plus(mat):
    n = mat.shape[0]
    rows = lax.broadcasted_iota(jnp.int32, (n, n), 0)
    cols = lax.broadcasted_iota(jnp.int32, (n, n), 1)
    return (jnp.where(rows == cols, 1.0, 0.0) + mat).astype(jnp.bfloat16)


def condition(raw, left_mat, right_mat, by_row, by_query, out):
    count = raw.shape[0]
    group = 16
    for a in range(0, FA, group):
        rows = jnp.concatenate([raw[:, i * FB:(i + 1) * FB] for i in range(a, a + group)], axis=0)
        mid = jnp.dot(rows, right_mat, preferred_element_type=jnp.float32).astype(jnp.bfloat16).astype(jnp.float32)
        for i in range(group):
            by_query[pl.ds(a + i, count, stride=FA), :] = mid[i * count:(i + 1) * count, :]
    group = 8
    for q in range(0, count, group):
        mid = jnp.concatenate([by_query[i * FA:(i + 1) * FA, :] for i in range(q, q + group)], axis=1)
        done = jnp.dot(left_mat, mid.astype(jnp.bfloat16), preferred_element_type=jnp.float32)
        for i in range(group):
            by_row[pl.ds(q + i, FA, stride=count), :] = done[:, i * FB:(i + 1) * FB]
    for a in range(FA):
        out[:, a * FB:(a + 1) * FB] = by_row[a * count:(a + 1) * count, :].astype(jnp.bfloat16)


def kernel(raw_ref, grads_ref, left_ref, right_ref, order_ref, out_ref, raw, left, right, order, by_row, by_query,
           grads, block, acc, tile, pick, scores, sums, halves, inbox, inbox_y, inbox_x, outbox, final,
           load_sem, main_recv, z_send, x_send, sib_send, sib_recv, red_send, red_recv, swap_send, swap_recv, fin_send, fin_recv):
    ex, me = lax.axis_index("ex"), lax.axis_index("layer")
    core = lax.rem(ex, 2)
    z = lax.rem(ex // 2, Z)
    hi = ex // (2 * Z)
    depth = block.shape[3]
    half, quarter, eighth = depth // 2, depth // 4, depth // 8
    main = depth - STRIP

    def at(h, zz, c):
        return h * (2 * Z) + zz * 2 + c

    toward = ((at(hi, lax.rem(z + 1, Z), core), me), (at(hi, lax.rem(z + Z - 1, Z), core), me))
    across = (at(1 - hi, z, core), me)
    sibling = (at(hi, z, 1 - core), me)

    y, lo = lax.rem(me, 4), me // 4
    aside = (ex, lax.rem(me + 4, GROUP))

    def peer_of(j):
        return ex, lax.rem(me + j + 1, GROUP)

    def along_y(j):
        return ex, lo * 4 + lax.rem(y + j + 1, 4)

    def rows_of(device):
        return 2 * lax.rem(device[1], 4) + device[1] // 4

    loads = [pltpu.make_async_copy(src, dst, load_sem.at[i]) for i, (src, dst) in enumerate(
        ((raw_ref, raw), (right_ref, right), (left_ref, left), (order_ref, order), (grads_ref, grads)))]
    for load in loads[:4]:
        load.start()

    barrier = pltpu.get_barrier_semaphore()
    for d in (*toward, across, sibling):
        pl.semaphore_signal(barrier, inc=1, device_id=d, device_id_type=MESH)

    @pl.loop(0, GROUP - 1)
    def _(j):
        pl.semaphore_signal(barrier, inc=1, device_id=peer_of(j), device_id_type=MESH)

    for load in loads[:3]:
        load.wait()
    mats = eye_plus(left[...]), eye_plus(right[...])
    condition(raw.at[0:16], *mats, by_row, by_query, block.at[0, core])

    def remote(src, dst, send_sem, recv_sem, device):
        return pltpu.make_async_remote_copy(src_ref=src, dst_ref=dst, send_sem=send_sem, recv_sem=recv_sem,
                                            device_id=device, device_id_type=MESH)

    def part(piece, c, start, width):
        if width == depth:
            return block.at[piece, c]
        return block.at[piece, c, :, pl.ds(start if isinstance(start, int) else pl.multiple_of(start, width), width)]

    def send(src, dst, start, width, send_sem, signal, device):
        remote(part(src, core, start, width), part(dst, core, start, width), send_sem, main_recv.at[signal], device).start()

    def arrived(piece, start, width, signal):
        here = part(piece, core, start, width)
        remote(here, here, z_send.at[0], main_recv.at[signal], sibling).wait_recv()

    def send_sib(piece, start, width, group):
        here = part(piece, core, start, width)
        remote(here, here, sib_send.at[group], sib_recv.at[group], sibling).start()

    def strip_of(step, way):
        return (main, STRIP) if step < 4 else (main + way * STRIP // 2, STRIP // 2)

    def last_part(k):
        if k < 6:
            return k * eighth, eighth
        return 6 * eighth + (k - 6) * (main - 6 * eighth) // 2, (main - 6 * eighth) // 2

    def strip_round_z(step, way):
        send(place("W", step, way), place("W", step + 1, way), *strip_of(step + 1, way), z_send.at[8 + step],
             STRIPS["W", step + 1, way], toward[way])

    def round_z(kind, step, way):
        src, dst = place(kind, step, way), place(kind, step + 1, way)
        device = toward[way]
        if kind == "N":
            start, width = (0, depth) if step < 3 else (way * half, half)
            send(src, dst, start, width, z_send.at[step], SECOND[dst] if step == 3 and way else dst, device)
            if step > 0:
                strip_round_z(step, way)
        elif step < 3:
            send(src, dst, 0, main, z_send.at[4 + step], dst, device)
        elif kind == "W":
            send(src, dst, way * main // 2, main // 2, z_send.at[4 + step], SECOND[dst] if way else dst, device)
        else:
            for k in range(way, 8, 2):
                send(src, dst, *last_part(k), z_send.at[4 + step], SECOND[dst] + k - 1 if k else dst, device)

    def over_x(kind, step, way):
        src, dst = place(kind, step, way), place("T" + kind, step, way)
        if kind == "W":
            send(src, dst, 0, main, x_send.at[0], dst, across)
            return
        start, width = (0, depth) if step < 4 else (way * half, half)
        send(src, dst, start, width, x_send.at[1 + step // 4], SECOND[dst] if step == 4 and way else dst, across)
        send(place("W", step, way), place("TW", step, way), *strip_of(step, way), x_send.at[3 + step // 4],
             STRIPS["TW", step, way], across)

    def take(kind, step, way):
        piece = place(kind, step, way)
        if kind[-1] == "W":
            start, width = (0, main) if step < 4 else (way * main // 2, main // 2)
        else:
            start, width = (0, depth) if step < 4 else (way * half, half)
        arrived(piece, start, width, SECOND[piece] if step == 4 and way else piece)
        send_sib(piece, start, width, batch_of(piece))
        if kind[-1] == "N":
            wide = kind[:-1] + "W"
            piece = place(wide, step, way)
            arrived(piece, *strip_of(step, way), STRIPS[wide, step, way])
            send_sib(piece, *strip_of(step, way), batch_of(piece) + 3 * (piece == FINAL))

    def sib_batch(b):
        first, count = BATCHES[b]
        count -= b == len(BATCHES) - 1
        here = block.at[first:first + count, 1 - core]
        return remote(here, here, sib_send.at[b], sib_recv.at[b], sibling)

    def sib_last(k):
        here = part(FINAL, 1 - core, k * quarter, quarter)
        sem = len(BATCHES) + k
        return remote(here, here, sib_send.at[sem], sib_recv.at[sem], sibling)

    def take_last(i):
        for k in (2 * i, 2 * i + 1):
            arrived(FINAL, *last_part(k), SECOND[FINAL] + k - 1 if k else FINAL)
            send_sib(FINAL, *last_part(k), len(BATCHES) + i)

    def product(first, count, start, width):
        cols = pl.ds(start if isinstance(start, int) else pl.multiple_of(start, width), width)
        rhs = block[first:first + count, :, :, cols].reshape(count * 32, width)
        return lax.dot_general(grads[:, cols], rhs, (((1,), (1,)), ((), ())), preferred_element_type=jnp.float32)

    def columns(b):
        return b * 256, 256

    def batch(b):
        first, count = BATCHES[b]
        sib_batch(b).wait_recv()
        w = count * 32
        acc[...] = jnp.zeros_like(acc)

        @pl.loop(0, 4)
        def _(k):
            if b == len(BATCHES) - 1:
                sib_last(k).wait_recv()
            acc[:, :w] += product(first, count, k * quarter, quarter)
            if b == len(BATCHES) - 1:
                pl.when(k == 0)(lambda: take_last(3))
        start, width = columns(b)
        tile[:, start:start + w] = acc[:, :w].astype(jnp.bfloat16)

        cols = slice(start, start + width)
        if b >= NEAR_SUMS:
            to = slice(start - NEAR_SUMS * 256, start - NEAR_SUMS * 256 + width)

            @pl.loop(0, GROUP - 1)
            def _(j):
                peer = peer_of(j)
                rows = pl.ds(pl.multiple_of(rows_of(peer) * 64, 64), 64)
                remote(tile.at[rows, cols], inbox.at[j, :, to], red_send.at[b], red_recv.at[b], peer).start()
        else:
            @pl.loop(0, 3)
            def _(j):
                peer = along_y(j)
                rows = pl.ds(pl.multiple_of(lax.rem(peer[1], 4) * 128, 128), 128)
                remote(tile.at[rows, cols], inbox_y.at[j, :, cols], red_send.at[b], red_recv.at[b], peer).start()

    def reduced(b):
        start, width = columns(b)
        late = start - NEAR_SUMS * 256
        here = inbox.at[:, :, late:late + width] if b >= NEAR_SUMS else inbox_y.at[:, :, start:start + width]
        return remote(here, here, red_send.at[b], red_recv.at[b], sibling)

    def swap_x(b):
        start, width = columns(b)
        cols = slice(start, start + width)
        reduced(b).wait_recv()
        total = tile[pl.ds(pl.multiple_of(y * 128, 128), 128), cols].astype(jnp.float32)
        for j in range(3):
            total += inbox_y[j, :, cols].astype(jnp.float32)
        for i in range(2):
            sums[i, :, cols] = total[i * 64:(i + 1) * 64]
            halves[i, :, cols] = total[i * 64:(i + 1) * 64].astype(jnp.bfloat16)
        remote(halves.at[1 - lo, :, cols], inbox_x.at[:, cols], swap_send.at[b], swap_recv.at[0], aside).start()

    def swapped(start, width, b):
        here = inbox_x.at[:, start:start + width]
        return remote(here, here, swap_send.at[b], swap_recv.at[0], sibling)

    pl.semaphore_wait(barrier, 4 + GROUP - 1)
    for way in WAYS:
        round_z("N", 0, way)
    condition(raw.at[16:32], *mats, by_row, by_query, block.at[1, core])
    over_x("W", 0, 0)
    for way in WAYS:
        strip_round_z(0, way)
        round_z("W", 0, way)
    for piece in (0, 1):
        send_sib(piece, 0, depth, 0)
    over_x("N", 0, 0)
    loads[4].start()

    loads[3].wait()
    row = lax.broadcasted_iota(jnp.int32, (32, 1), 0)
    row = row + 16 * (row // 16)

    def first_query(piece):
        kind, step, way = PIECES[piece]
        zz = lax.rem(z + (Z - step if way == FWD else step), Z)
        hh = 1 - hi if kind[0] == "T" else hi
        return (hh * Z + zz) * 64 + (16 if kind[-1] == "W" else 0)

    for piece in range(len(PIECES)):
        rows = slice(piece * 32, (piece + 1) * 32)
        pick[rows, :] = jnp.where(row + first_query(piece) == order[...], 1.0, 0.0).astype(jnp.bfloat16)
    def ordered(total, start):
        high = total.astype(jnp.bfloat16)
        low = (total - high.astype(jnp.float32)).astype(jnp.bfloat16)
        both = jnp.dot(jnp.concatenate([high, low], axis=0), pick[start:start + total.shape[1], :],
                       preferred_element_type=jnp.float32)
        return both[:64] + both[64:]

    def late_sum(b):
        start, width = columns(b)
        reduced(b).wait_recv()
        total = tile[pl.ds(pl.multiple_of(rows_of((ex, me)) * 64, 64), 64), start:start + width].astype(jnp.float32)
        for j in range(GROUP - 1):
            total += inbox[j, :, start - NEAR_SUMS * 256:start - NEAR_SUMS * 256 + width].astype(jnp.float32)
        return ordered(total, start)

    for way in WAYS:
        take("N", 1, way)
        round_z("N", 1, way)
    for way in WAYS:
        over_x("N", 1, way)
    take("TW", 0, 0)
    for way in WAYS:
        round_z("TW", 0, way)
    for way in WAYS:
        take("W", 1, way)
    take("TN", 0, 0)
    loads[4].wait()
    batch(0)
    for way in WAYS:
        take("N", 2, way)
        round_z("N", 2, way)
        over_x("N", 2, way)
    for way in WAYS:
        round_z("W", 1, way)
    for kind in ("TW", "TN"):
        for way in WAYS:
            take(kind, 1, way)
    for way in WAYS:
        take("N", 3, way)
        round_z("N", 3, way)
        over_x("N", 3, way)
    for way in WAYS:
        round_z("TW", 1, way)
    batch(1)
    for way in WAYS:
        take("W", 2, way)
        round_z("W", 2, way)
    for way in WAYS:
        take("N", 4, way)
        over_x("N", 4, way)
    for way in WAYS:
        take("TN", 2, way)
    for way in WAYS:
        take("TW", 2, way)
        round_z("TW", 2, way)
    for way in WAYS:
        take("W", 3, way)
        round_z("W", 3, way)
    swap_x(0)
    swap_x(1)
    batch(2)
    for way in WAYS:
        take("TN", 3, way)
    for way in WAYS:
        take("TW", 3, way)
        round_z("TW", 3, way)
    for kind in ("W", "TN"):
        for way in WAYS:
            take(kind, 4, way)
    for i in range(3):
        take_last(i)
    swap_x(2)
    batch(3)
    swapped(0, NEAR_SUMS * 256, 0).wait_recv()
    scores[...] = ordered(sums[lo] + inbox_x[...].astype(jnp.float32), 0)
    done = (scores[...] + late_sum(3)).astype(jnp.bfloat16)
    for m in range(GROUP):
        outbox[m] = done[:, m * 128:(m + 1) * 128]

    @pl.loop(0, GROUP - 1)
    def _(j):
        peer = peer_of(j)
        remote(outbox.at[peer[1]], final.at[rows_of((ex, me))], fin_send.at[0], fin_recv.at[0], peer).start()
    final[rows_of((ex, me))] = outbox[me]

    def units(n, width, sem):
        here = block.at[0:n, core, :, 0:width]
        remote(here, here, sem, main_recv.at[0], sibling).wait_send()

    for step in range(4):
        parts = 1 if step < 3 else 2
        units(2, depth // parts, z_send.at[step])
        units(4, main // parts, z_send.at[4 + step])
        units(2, STRIP // parts, z_send.at[8 + step])
    for sem, (n, width) in enumerate(((1, main), (7, depth), (2, half), (7, STRIP), (2, STRIP // 2))):
        units(n, width, x_send.at[sem])
    for b in range(len(BATCHES)):
        sib_batch(b).wait_send()
        reduced(b).wait_send()
    for b in range(NEAR_SUMS):
        swapped(0, 256, b).wait_send()
    for k in range(4):
        sib_last(k).wait_send()
    whole = remote(final.at[0:GROUP - 1], final.at[0:GROUP - 1], fin_send.at[0], fin_recv.at[0], sibling)
    whole.wait_send()
    whole.wait_recv()
    out_ref[...] = final[...].reshape(out_ref.shape).astype(jnp.float32) * (1.0 / 256.0)


def local(train_grads, query_grads, left_factor, right_factor, query_order):
    grads = train_grads[:, 0, :]
    raw = query_grads[:, 0, :]
    rows, depth = grads.shape
    own = raw.shape[0]
    queries = query_order.shape[0]
    dma = pltpu.SemaphoreType.DMA
    return pl.pallas_call(
        kernel,
        name="scores",
        out_shape=jax.ShapeDtypeStruct((rows, queries // GROUP), jnp.float32),
        in_specs=[pl.BlockSpec(memory_space=pl.ANY)] * 5,
        out_specs=pl.BlockSpec(memory_space=pltpu.VMEM),
        scratch_shapes=[
            pltpu.VMEM((own, depth), jnp.bfloat16),
            pltpu.VMEM((FA, FA), jnp.float32),
            pltpu.VMEM((FB, FB), jnp.float32),
            pltpu.VMEM((1, queries), jnp.int32),
            pltpu.VMEM((own * FA, FB), jnp.float32),
            pltpu.VMEM((own * FA, FB), jnp.float32),
            pltpu.VMEM((rows, depth), jnp.bfloat16),
            pltpu.VMEM((len(PIECES), 2, own // 2, depth), jnp.bfloat16),
            pltpu.VMEM((rows, 256), jnp.float32),
            pltpu.VMEM((rows, COLUMNS), jnp.bfloat16),
            pltpu.VMEM((COLUMNS, queries), jnp.bfloat16),
            pltpu.VMEM((rows // GROUP, queries), jnp.float32),
            pltpu.VMEM((2, rows // GROUP, NEAR_SUMS * 256), jnp.float32),
            pltpu.VMEM((2, rows // GROUP, NEAR_SUMS * 256), jnp.bfloat16),
            pltpu.VMEM((GROUP - 1, rows // GROUP, COLUMNS - NEAR_SUMS * 256), jnp.bfloat16),
            pltpu.VMEM((3, rows // 4, NEAR_SUMS * 256), jnp.bfloat16),
            pltpu.VMEM((rows // GROUP, NEAR_SUMS * 256), jnp.bfloat16),
            pltpu.VMEM((GROUP, rows // GROUP, queries // GROUP), jnp.bfloat16),
            pltpu.VMEM((GROUP, rows // GROUP, queries // GROUP), jnp.bfloat16),
            dma((5,)),
            dma((ARRIVALS,)),
            dma((12,)),
            dma((5,)),
            dma((len(BATCHES) + 4,)),
            dma((len(BATCHES) + 4,)),
            dma((len(BATCHES),)),
            dma((len(BATCHES),)),
            dma((NEAR_SUMS,)),
            dma((1,)),
            dma((1,)),
            dma((1,)),
        ],
        compiler_params=pltpu.CompilerParams(
            collective_id=0, has_side_effects=True, vmem_limit_bytes=52 * 2**20
        ),
        cost_estimate=pl.CostEstimate(
            flops=2 * rows * depth * queries, bytes_accessed=rows * depth * 2, transcendentals=0
        ),
    )(*(pltpu.with_memory_space_constraint(x, pltpu.HBM) for x in (
        raw, grads, left_factor[0], right_factor[0], query_order.reshape(1, queries))))


def solution(mesh):
    return jax.shard_map(
        local,
        mesh=mesh,
        in_specs=(
            P("ex", "layer", None),
            P("ex", "layer", None),
            P("layer", None, None),
            P("layer", None, None),
            P(),
        ),
        out_specs=P("ex", "layer"),
        check_vma=False,
    )
```

```python
import functools

import jax
import jax.numpy as jnp
from jax import lax
from jax.experimental import pallas as pl
from jax.experimental.pallas import tpu as pltpu
from jax.sharding import PartitionSpec as P

FA = 64
FB = 128
MESH = pl.DeviceIdType.MESH

Z = 8
GROUP = 8
FWD, BWD = 0, 1
WAYS = (FWD, BWD)

PIECES = (
    ("N", 0, 0), ("W", 0, 0), ("TW", 0, 0), ("TN", 0, 0), ("N", 1, 0), ("N", 1, 1), ("W", 1, 0), ("W", 1, 1),
    ("N", 2, 0), ("N", 2, 1), ("TW", 1, 0), ("TW", 1, 1), ("TN", 1, 0), ("TN", 1, 1), ("N", 3, 0), ("N", 3, 1),
    ("W", 2, 0), ("W", 2, 1), ("TN", 2, 0), ("TN", 2, 1), ("N", 4, 0), ("TW", 2, 0), ("TW", 2, 1), ("W", 3, 0),
    ("TN", 3, 0), ("TN", 3, 1), ("W", 3, 1), ("TW", 3, 0), ("TW", 3, 1), ("TN", 4, 0), ("W", 4, 0), ("TW", 4, 0),
)
BATCHES = ((0, 8), (8, 8), (16, 8), (24, 8))
FINAL = 31
NEAR_SUMS = 3
COLUMNS = 32 * len(PIECES)


def place(kind, step, way):
    return PIECES.index((kind, step, way if 0 < step < 4 else 0))


def batch_of(piece):
    return len(BATCHES) if piece == FINAL else piece // 8


STRIP = 768

SECOND = {place("N", 4, 0): 32, place("W", 4, 0): 33, place("TN", 4, 0): 34, FINAL: 35}
STRIPS = {}
for kind in ("W", "TW"):
    for step in range(kind == "W", 5):
        for way in WAYS if step else (FWD,):
            STRIPS[kind, step, way] = 42 + len(STRIPS)
ARRIVALS = 42 + len(STRIPS)


def eye_plus(mat):
    n = mat.shape[0]
    rows = lax.broadcasted_iota(jnp.int32, (n, n), 0)
    cols = lax.broadcasted_iota(jnp.int32, (n, n), 1)
    return (jnp.where(rows == cols, 1.0, 0.0) + mat).astype(jnp.bfloat16)


def condition(raw, left_mat, right_mat, by_row, by_query, out):
    count = raw.shape[0]
    group = 16
    for a in range(0, FA, group):
        rows = jnp.concatenate([raw[:, i * FB:(i + 1) * FB] for i in range(a, a + group)], axis=0)
        mid = jnp.dot(rows, right_mat, preferred_element_type=jnp.float32).astype(jnp.bfloat16).astype(jnp.float32)
        for i in range(group):
            by_query[pl.ds(a + i, count, stride=FA), :] = mid[i * count:(i + 1) * count, :]
    group = 8
    for q in range(0, count, group):
        mid = jnp.concatenate([by_query[i * FA:(i + 1) * FA, :] for i in range(q, q + group)], axis=1)
        done = jnp.dot(left_mat, mid.astype(jnp.bfloat16), preferred_element_type=jnp.float32)
        for i in range(group):
            by_row[pl.ds(q + i, FA, stride=count), :] = done[:, i * FB:(i + 1) * FB]
    for a in range(FA):
        out[:, a * FB:(a + 1) * FB] = by_row[a * count:(a + 1) * count, :].astype(jnp.bfloat16)


def kernel(raw_ref, grads_ref, left_ref, right_ref, order_ref, out_ref, raw, left, right, order, by_row, by_query,
           grads, block, acc, tile, pick, scores, sums, halves, inbox, inbox_y, inbox_x, outbox, final,
           load_sem, main_recv, z_send, x_send, sib_send, sib_recv, red_send, red_recv, swap_send, swap_recv, fin_send, fin_recv):
    ex, me = lax.axis_index("ex"), lax.axis_index("layer")
    core = lax.rem(ex, 2)
    z = lax.rem(ex // 2, Z)
    hi = ex // (2 * Z)
    depth = block.shape[3]
    half, quarter, eighth = depth // 2, depth // 4, depth // 8
    main = depth - STRIP

    def at(h, zz, c):
        return h * (2 * Z) + zz * 2 + c

    toward = ((at(hi, lax.rem(z + 1, Z), core), me), (at(hi, lax.rem(z + Z - 1, Z), core), me))
    across = (at(1 - hi, z, core), me)
    sibling = (at(hi, z, 1 - core), me)

    y, lo = lax.rem(me, 4), me // 4
    aside = (ex, lax.rem(me + 4, GROUP))

    def peer_of(j):
        return ex, lax.rem(me + j + 1, GROUP)

    def along_y(j):
        return ex, lo * 4 + lax.rem(y + j + 1, 4)

    def rows_of(device):
        return 2 * lax.rem(device[1], 4) + device[1] // 4

    loads = [pltpu.make_async_copy(src, dst, load_sem.at[i]) for i, (src, dst) in enumerate(
        ((raw_ref, raw), (right_ref, right), (left_ref, left), (order_ref, order), (grads_ref, grads)))]
    for load in loads[:4]:
        load.start()

    barrier = pltpu.get_barrier_semaphore()
    for d in (*toward, across, sibling):
        pl.semaphore_signal(barrier, inc=1, device_id=d, device_id_type=MESH)

    @pl.loop(0, GROUP - 1)
    def _(j):
        pl.semaphore_signal(barrier, inc=1, device_id=peer_of(j), device_id_type=MESH)

    for load in loads[:3]:
        load.wait()
    mats = eye_plus(left[...]), eye_plus(right[...])
    condition(raw.at[0:16], *mats, by_row, by_query, block.at[0, core])

    def remote(src, dst, send_sem, recv_sem, device):
        return pltpu.make_async_remote_copy(src_ref=src, dst_ref=dst, send_sem=send_sem, recv_sem=recv_sem,
                                            device_id=device, device_id_type=MESH)

    def part(piece, c, start, width):
        if width == depth:
            return block.at[piece, c]
        return block.at[piece, c, :, pl.ds(start if isinstance(start, int) else pl.multiple_of(start, width), width)]

    def send(src, dst, start, width, send_sem, signal, device):
        remote(part(src, core, start, width), part(dst, core, start, width), send_sem, main_recv.at[signal], device).start()

    def arrived(piece, start, width, signal):
        here = part(piece, core, start, width)
        remote(here, here, z_send.at[0], main_recv.at[signal], sibling).wait_recv()

    def send_sib(piece, start, width, group):
        here = part(piece, core, start, width)
        remote(here, here, sib_send.at[min(group, len(BATCHES))], sib_recv.at[group], sibling).start()

    def strip_of(step, way):
        return (main, STRIP) if step < 4 else (main + way * STRIP // 2, STRIP // 2)

    def last_part(k):
        if k < 6:
            return k * eighth, eighth
        return 6 * eighth + (k - 6) * (main - 6 * eighth) // 2, (main - 6 * eighth) // 2

    def strip_round_z(step, way):
        send(place("W", step, way), place("W", step + 1, way), *strip_of(step + 1, way), z_send.at[2],
             STRIPS["W", step + 1, way], toward[way])

    def round_z(kind, step, way):
        src, dst = place(kind, step, way), place(kind, step + 1, way)
        device = toward[way]
        if kind == "N":
            start, width = (0, depth) if step < 3 else (way * half, half)
            send(src, dst, start, width, z_send.at[0], SECOND[dst] if step == 3 and way else dst, device)
            if step > 0:
                strip_round_z(step, way)
        elif step < 3:
            send(src, dst, 0, main, z_send.at[1], dst, device)
        elif kind == "W":
            send(src, dst, way * main // 2, main // 2, z_send.at[1], SECOND[dst] if way else dst, device)
        else:
            for k in range(way, 8, 2):
                send(src, dst, *last_part(k), z_send.at[1], SECOND[dst] + k - 1 if k else dst, device)

    def over_x(kind, step, way):
        src, dst = place(kind, step, way), place("T" + kind, step, way)
        if kind == "W":
            send(src, dst, 0, main, x_send.at[0], dst, across)
            return
        start, width = (0, depth) if step < 4 else (way * half, half)
        send(src, dst, start, width, x_send.at[1], SECOND[dst] if step == 4 and way else dst, across)
        send(place("W", step, way), place("TW", step, way), *strip_of(step, way), x_send.at[2],
             STRIPS["TW", step, way], across)

    def take(kind, step, way, *onward):
        piece = place(kind, step, way)
        if kind[-1] == "W":
            start, width = (0, main) if step < 4 else (way * main // 2, main // 2)
        else:
            start, width = (0, depth) if step < 4 else (way * half, half)
        arrived(piece, start, width, SECOND[piece] if step == 4 and way else piece)
        wide = place(kind[:-1] + "W", step, way)
        if kind[-1] == "N":
            arrived(wide, *strip_of(step, way), STRIPS[kind[:-1] + "W", step, way])
        for go in onward:
            go(kind, step, way)
        send_sib(piece, start, width, batch_of(piece))
        if kind[-1] == "N":
            send_sib(wide, *strip_of(step, way), batch_of(wide) + 3 * (wide == FINAL))

    def sib_batch(b):
        first, count = BATCHES[b]
        count -= b == len(BATCHES) - 1
        here = block.at[first:first + count, 1 - core]
        return remote(here, here, sib_send.at[b], sib_recv.at[b], sibling)

    def sib_last(k):
        here = part(FINAL, 1 - core, k * quarter, quarter)
        sem = len(BATCHES) + k
        return remote(here, here, sib_send.at[len(BATCHES)], sib_recv.at[sem], sibling)

    def take_last(i):
        for k in (2 * i, 2 * i + 1):
            arrived(FINAL, *last_part(k), SECOND[FINAL] + k - 1 if k else FINAL)
            send_sib(FINAL, *last_part(k), len(BATCHES) + i)

    def product(first, count, start, width):
        cols = pl.ds(start if isinstance(start, int) else pl.multiple_of(start, width), width)
        rhs = block[first:first + count, :, :, cols].reshape(count * 32, width)
        return lax.dot_general(grads[:, cols], rhs, (((1,), (1,)), ((), ())), preferred_element_type=jnp.float32)

    def columns(b):
        return b * 256, 256

    def batch(b):
        first, count = BATCHES[b]
        sib_batch(b).wait_recv()
        w = count * 32
        acc[...] = jnp.zeros_like(acc)

        @pl.loop(0, 4)
        def _(k):
            if b == len(BATCHES) - 1:
                sib_last(k).wait_recv()
            acc[:, :w] += product(first, count, k * quarter, quarter)
            if b == len(BATCHES) - 1:
                pl.when(k == 0)(lambda: take_last(3))
        start, width = columns(b)
        tile[:, start:start + w] = acc[:, :w].astype(jnp.bfloat16)

        cols = slice(start, start + width)
        if b >= NEAR_SUMS:
            to = slice(start - NEAR_SUMS * 256, start - NEAR_SUMS * 256 + width)

            @pl.loop(0, GROUP - 1)
            def _(j):
                peer = peer_of(j)
                rows = pl.ds(pl.multiple_of(rows_of(peer) * 64, 64), 64)
                remote(tile.at[rows, cols], inbox.at[j, :, to], red_send.at[b], red_recv.at[b], peer).start()
        else:
            @pl.loop(0, 3)
            def _(j):
                peer = along_y(j)
                rows = pl.ds(pl.multiple_of(lax.rem(peer[1], 4) * 128, 128), 128)
                remote(tile.at[rows, cols], inbox_y.at[j, :, cols], red_send.at[b], red_recv.at[b], peer).start()

    def reduced(b):
        start, width = columns(b)
        late = start - NEAR_SUMS * 256
        here = inbox.at[:, :, late:late + width] if b >= NEAR_SUMS else inbox_y.at[:, :, start:start + width]
        return remote(here, here, red_send.at[b], red_recv.at[b], sibling)

    def swap_x(b):
        start, width = columns(b)
        cols = slice(start, start + width)
        reduced(b).wait_recv()
        total = tile[pl.ds(pl.multiple_of(y * 128, 128), 128), cols].astype(jnp.float32)
        for j in range(3):
            total += inbox_y[j, :, cols].astype(jnp.float32)
        for i in range(2):
            sums[i, :, cols] = total[i * 64:(i + 1) * 64]
            halves[i, :, cols] = total[i * 64:(i + 1) * 64].astype(jnp.bfloat16)
        remote(halves.at[1 - lo, :, cols], inbox_x.at[:, cols], swap_send.at[b], swap_recv.at[0], aside).start()

    def swapped(start, width, b):
        here = inbox_x.at[:, start:start + width]
        return remote(here, here, swap_send.at[b], swap_recv.at[0], sibling)

    pl.semaphore_wait(barrier, 4 + GROUP - 1)
    for way in WAYS:
        round_z("N", 0, way)
    condition(raw.at[16:32], *mats, by_row, by_query, block.at[1, core])
    over_x("W", 0, 0)
    for way in WAYS:
        strip_round_z(0, way)
        round_z("W", 0, way)
    over_x("N", 0, 0)
    loads[4].start()

    loads[3].wait()
    row = lax.broadcasted_iota(jnp.int32, (32, 1), 0)
    row = row + 16 * (row // 16)

    def first_query(piece):
        kind, step, way = PIECES[piece]
        zz = lax.rem(z + (Z - step if way == FWD else step), Z)
        hh = 1 - hi if kind[0] == "T" else hi
        return (hh * Z + zz) * 64 + (16 if kind[-1] == "W" else 0)

    for piece in range(len(PIECES)):
        rows = slice(piece * 32, (piece + 1) * 32)
        pick[rows, :] = jnp.where(row + first_query(piece) == order[...], 1.0, 0.0).astype(jnp.bfloat16)
    def ordered(total, start):
        high = total.astype(jnp.bfloat16)
        low = (total - high.astype(jnp.float32)).astype(jnp.bfloat16)
        both = jnp.dot(jnp.concatenate([high, low], axis=0), pick[start:start + total.shape[1], :],
                       preferred_element_type=jnp.float32)
        return both[:64] + both[64:]

    def late_sum(b):
        start, width = columns(b)
        reduced(b).wait_recv()
        total = tile[pl.ds(pl.multiple_of(rows_of((ex, me)) * 64, 64), 64), start:start + width].astype(jnp.float32)
        for j in range(GROUP - 1):
            total += inbox[j, :, start - NEAR_SUMS * 256:start - NEAR_SUMS * 256 + width].astype(jnp.float32)
        return ordered(total, start)

    for way in WAYS:
        take("N", 1, way, round_z)
    for way in WAYS:
        over_x("N", 1, way)
    for piece in (0, 1):
        send_sib(piece, 0, depth, 0)
    take("TW", 0, 0)
    for way in WAYS:
        round_z("TW", 0, way)
    for way in WAYS:
        take("W", 1, way)
    take("TN", 0, 0)
    loads[4].wait()
    batch(0)
    for way in WAYS:
        take("N", 2, way, round_z, over_x)
    for way in WAYS:
        round_z("W", 1, way)
    for kind in ("TW", "TN"):
        for way in WAYS:
            take(kind, 1, way)
    for way in WAYS:
        take("N", 3, way, round_z, over_x)
    for way in WAYS:
        round_z("TW", 1, way)
    batch(1)
    for way in WAYS:
        take("W", 2, way, round_z)
    for way in WAYS:
        take("N", 4, way, over_x)
    for way in WAYS:
        take("TN", 2, way)
    for way in WAYS:
        take("TW", 2, way, round_z)
    for way in WAYS:
        take("W", 3, way, round_z)
    batch(2)
    for way in WAYS:
        take("TN", 3, way)
    for way in WAYS:
        take("TW", 3, way, round_z)
    for kind in ("W", "TN"):
        for way in WAYS:
            take(kind, 4, way)
    for i in range(3):
        take_last(i)
    for b in range(NEAR_SUMS):
        swap_x(b)
    batch(3)
    swapped(0, NEAR_SUMS * 256, 0).wait_recv()
    scores[...] = ordered(sums[lo] + inbox_x[...].astype(jnp.float32), 0)
    done = (scores[...] + late_sum(3)).astype(jnp.bfloat16)
    for m in range(GROUP):
        outbox[m] = done[:, m * 128:(m + 1) * 128]

    @pl.loop(0, GROUP - 1)
    def _(j):
        peer = peer_of(j)
        remote(outbox.at[peer[1]], final.at[rows_of((ex, me))], fin_send.at[0], fin_recv.at[0], peer).start()
    final[rows_of((ex, me))] = outbox[me]

    def units(n, width, sem):
        here = block.at[0:n, core, :, 0:width]
        remote(here, here, sem, main_recv.at[0], sibling).wait_send()

    for sem, (n, width) in enumerate(((7, depth), (14, main), (7, STRIP))):
        units(n, width, z_send.at[sem])
    for sem, (n, width) in enumerate(((1, main), (8, depth), (8, STRIP))):
        units(n, width, x_send.at[sem])
    for b in range(len(BATCHES)):
        sib_batch(b).wait_send()
        reduced(b).wait_send()
    for b in range(NEAR_SUMS):
        swapped(0, 256, b).wait_send()
    units(1, depth, sib_send.at[len(BATCHES)])
    whole = remote(final.at[0:GROUP - 1], final.at[0:GROUP - 1], fin_send.at[0], fin_recv.at[0], sibling)
    whole.wait_send()
    whole.wait_recv()
    out_ref[...] = final[...].reshape(out_ref.shape).astype(jnp.float32) * (1.0 / 256.0)


def local(train_grads, query_grads, left_factor, right_factor, query_order):
    grads = train_grads[:, 0, :]
    raw = query_grads[:, 0, :]
    rows, depth = grads.shape
    own = raw.shape[0]
    queries = query_order.shape[0]
    dma = pltpu.SemaphoreType.DMA
    return pl.pallas_call(
        kernel,
        name="scores",
        out_shape=jax.ShapeDtypeStruct((rows, queries // GROUP), jnp.float32),
        in_specs=[pl.BlockSpec(memory_space=pl.ANY)] * 5,
        out_specs=pl.BlockSpec(memory_space=pltpu.VMEM),
        scratch_shapes=[
            pltpu.VMEM((own, depth), jnp.bfloat16),
            pltpu.VMEM((FA, FA), jnp.float32),
            pltpu.VMEM((FB, FB), jnp.float32),
            pltpu.VMEM((1, queries), jnp.int32),
            pltpu.VMEM((own * FA, FB), jnp.float32),
            pltpu.VMEM((own * FA, FB), jnp.float32),
            pltpu.VMEM((rows, depth), jnp.bfloat16),
            pltpu.VMEM((len(PIECES), 2, own // 2, depth), jnp.bfloat16),
            pltpu.VMEM((rows, 256), jnp.float32),
            pltpu.VMEM((rows, COLUMNS), jnp.bfloat16),
            pltpu.VMEM((COLUMNS, queries), jnp.bfloat16),
            pltpu.VMEM((rows // GROUP, queries), jnp.float32),
            pltpu.VMEM((2, rows // GROUP, NEAR_SUMS * 256), jnp.float32),
            pltpu.VMEM((2, rows // GROUP, NEAR_SUMS * 256), jnp.bfloat16),
            pltpu.VMEM((GROUP - 1, rows // GROUP, COLUMNS - NEAR_SUMS * 256), jnp.bfloat16),
            pltpu.VMEM((3, rows // 4, NEAR_SUMS * 256), jnp.bfloat16),
            pltpu.VMEM((rows // GROUP, NEAR_SUMS * 256), jnp.bfloat16),
            pltpu.VMEM((GROUP, rows // GROUP, queries // GROUP), jnp.bfloat16),
            pltpu.VMEM((GROUP, rows // GROUP, queries // GROUP), jnp.bfloat16),
            dma((5,)),
            dma((ARRIVALS,)),
            dma((3,)),
            dma((3,)),
            dma((len(BATCHES) + 1,)),
            dma((len(BATCHES) + 4,)),
            dma((len(BATCHES),)),
            dma((len(BATCHES),)),
            dma((NEAR_SUMS,)),
            dma((1,)),
            dma((1,)),
            dma((1,)),
        ],
        compiler_params=pltpu.CompilerParams(
            collective_id=0, has_side_effects=True, vmem_limit_bytes=52 * 2**20
        ),
        cost_estimate=pl.CostEstimate(
            flops=2 * rows * depth * queries, bytes_accessed=rows * depth * 2, transcendentals=0
        ),
    )(*(pltpu.with_memory_space_constraint(x, pltpu.HBM) for x in (
        raw, grads, left_factor[0], right_factor[0], query_order.reshape(1, queries))))


def solution(mesh):
    return jax.shard_map(
        local,
        mesh=mesh,
        in_specs=(
            P("ex", "layer", None),
            P("ex", "layer", None),
            P("layer", None, None),
            P("layer", None, None),
            P(),
        ),
        out_specs=P("ex", "layer"),
        check_vma=False,
    )
```

```python
import functools

import jax
import jax.numpy as jnp
from jax import lax
from jax.experimental import pallas as pl
from jax.experimental.pallas import tpu as pltpu
from jax.sharding import PartitionSpec as P

FA = 64
FB = 128
MESH = pl.DeviceIdType.MESH

Z = 8
GROUP = 8
FWD, BWD = 0, 1
WAYS = (FWD, BWD)

PIECES = (
    ("N", 0, 0), ("W", 0, 0), ("TW", 0, 0), ("TN", 0, 0), ("N", 1, 0), ("N", 1, 1), ("W", 1, 0), ("W", 1, 1),
    ("N", 2, 0), ("N", 2, 1), ("TW", 1, 0), ("TW", 1, 1), ("TN", 1, 0), ("TN", 1, 1), ("N", 3, 0), ("N", 3, 1),
    ("W", 2, 0), ("W", 2, 1), ("TN", 2, 0), ("TN", 2, 1), ("N", 4, 0), ("TW", 2, 0), ("TW", 2, 1), ("W", 3, 0),
    ("TN", 3, 0), ("TN", 3, 1), ("W", 3, 1), ("TW", 3, 0), ("TW", 3, 1), ("TN", 4, 0), ("W", 4, 0), ("TW", 4, 0),
)
BATCHES = ((0, 8), (8, 8), (16, 8), (24, 8))
FINAL = 31
NEAR_SUMS = 3
COLUMNS = 32 * len(PIECES)


def place(kind, step, way):
    return PIECES.index((kind, step, way if 0 < step < 4 else 0))


def batch_of(piece):
    return len(BATCHES) if piece == FINAL else piece // 8


STRIP = 768

SECOND = {place("N", 4, 0): 32, place("W", 4, 0): 33, place("TN", 4, 0): 34, FINAL: 35}
STRIPS = {}
for kind in ("W", "TW"):
    for step in range(kind == "W", 5):
        for way in WAYS if step else (FWD,):
            STRIPS[kind, step, way] = 42 + len(STRIPS)
ARRIVALS = 42 + len(STRIPS)


def eye_plus(mat):
    n = mat.shape[0]
    rows = lax.broadcasted_iota(jnp.int32, (n, n), 0)
    cols = lax.broadcasted_iota(jnp.int32, (n, n), 1)
    return (jnp.where(rows == cols, 1.0, 0.0) + mat).astype(jnp.bfloat16)


def condition(raw, left_mat, right_mat, by_row, by_query, out):
    count = raw.shape[0]
    group = 16
    for a in range(0, FA, group):
        rows = jnp.concatenate([raw[:, i * FB:(i + 1) * FB] for i in range(a, a + group)], axis=0)
        mid = jnp.dot(rows, right_mat, preferred_element_type=jnp.float32).astype(jnp.bfloat16).astype(jnp.float32)
        for i in range(group):
            by_query[pl.ds(a + i, count, stride=FA), :] = mid[i * count:(i + 1) * count, :]
    group = 8
    for q in range(0, count, group):
        mid = jnp.concatenate([by_query[i * FA:(i + 1) * FA, :] for i in range(q, q + group)], axis=1)
        done = jnp.dot(left_mat, mid.astype(jnp.bfloat16), preferred_element_type=jnp.float32)
        for i in range(group):
            by_row[pl.ds(q + i, FA, stride=count), :] = done[:, i * FB:(i + 1) * FB]
    for a in range(FA):
        out[:, a * FB:(a + 1) * FB] = by_row[a * count:(a + 1) * count, :].astype(jnp.bfloat16)


def kernel(raw_ref, grads_ref, left_ref, right_ref, order_ref, out_ref, raw, left, right, order, by_row, by_query,
           grads, block, acc, tile, pick, scores, sums, halves, inbox, inbox_y, inbox_x, outbox, final,
           load_sem, main_recv, z_send, x_send, sib_send, sib_recv, red_send, red_recv, swap_send, swap_recv, fin_send, fin_recv):
    ex, me = lax.axis_index("ex"), lax.axis_index("layer")
    core = lax.rem(ex, 2)
    z = lax.rem(ex // 2, Z)
    hi = ex // (2 * Z)
    depth = block.shape[3]
    half, quarter, eighth = depth // 2, depth // 4, depth // 8
    main = depth - STRIP

    def at(h, zz, c):
        return h * (2 * Z) + zz * 2 + c

    toward = ((at(hi, lax.rem(z + 1, Z), core), me), (at(hi, lax.rem(z + Z - 1, Z), core), me))
    across = (at(1 - hi, z, core), me)
    sibling = (at(hi, z, 1 - core), me)

    y, lo = lax.rem(me, 4), me // 4
    aside = (ex, lax.rem(me + 4, GROUP))

    def peer_of(j):
        return ex, lax.rem(me + j + 1, GROUP)

    def along_y(j):
        return ex, lo * 4 + lax.rem(y + j + 1, 4)

    def rows_of(device):
        return 2 * lax.rem(device[1], 4) + device[1] // 4

    loads = [pltpu.make_async_copy(src, dst, load_sem.at[i]) for i, (src, dst) in enumerate(
        ((raw_ref, raw), (right_ref, right), (left_ref, left), (order_ref, order), (grads_ref, grads)))]
    for load in loads[:4]:
        load.start()

    barrier = pltpu.get_barrier_semaphore()
    for d in (*toward, across, sibling):
        pl.semaphore_signal(barrier, inc=1, device_id=d, device_id_type=MESH)

    @pl.loop(0, GROUP - 1)
    def _(j):
        pl.semaphore_signal(barrier, inc=1, device_id=peer_of(j), device_id_type=MESH)

    for load in loads[:3]:
        load.wait()
    mats = eye_plus(left[...]), eye_plus(right[...])
    condition(raw.at[0:16], *mats, by_row, by_query, block.at[0, core])

    def remote(src, dst, send_sem, recv_sem, device):
        return pltpu.make_async_remote_copy(src_ref=src, dst_ref=dst, send_sem=send_sem, recv_sem=recv_sem,
                                            device_id=device, device_id_type=MESH)

    def part(piece, c, start, width):
        if width == depth:
            return block.at[piece, c]
        return block.at[piece, c, :, pl.ds(start if isinstance(start, int) else pl.multiple_of(start, width), width)]

    def send(src, dst, start, width, send_sem, signal, device):
        remote(part(src, core, start, width), part(dst, core, start, width), send_sem, main_recv.at[signal], device).start()

    def arrived(piece, start, width, signal):
        here = part(piece, core, start, width)
        remote(here, here, z_send.at[0], main_recv.at[signal], sibling).wait_recv()

    def send_sib(piece, start, width, group):
        here = part(piece, core, start, width)
        remote(here, here, sib_send.at[group], sib_recv.at[group], sibling).start()

    def strip_of(step, way):
        return (main, STRIP) if step < 4 else (main + way * STRIP // 2, STRIP // 2)

    def last_part(k):
        if k < 6:
            return k * eighth, eighth
        return 6 * eighth + (k - 6) * (main - 6 * eighth) // 2, (main - 6 * eighth) // 2

    def strip_round_z(step, way):
        send(place("W", step, way), place("W", step + 1, way), *strip_of(step + 1, way), z_send.at[8 + step],
             STRIPS["W", step + 1, way], toward[way])

    def round_z(kind, step, way):
        src, dst = place(kind, step, way), place(kind, step + 1, way)
        device = toward[way]
        if kind == "N":
            start, width = (0, depth) if step < 3 else (way * half, half)
            send(src, dst, start, width, z_send.at[step], SECOND[dst] if step == 3 and way else dst, device)
            if step > 0:
                strip_round_z(step, way)
        elif step < 3:
            send(src, dst, 0, main, z_send.at[4 + step], dst, device)
        elif kind == "W":
            send(src, dst, way * main // 2, main // 2, z_send.at[4 + step], SECOND[dst] if way else dst, device)
        else:
            for k in range(way, 8, 2):
                send(src, dst, *last_part(k), z_send.at[4 + step], SECOND[dst] + k - 1 if k else dst, device)

    def over_x(kind, step, way):
        src, dst = place(kind, step, way), place("T" + kind, step, way)
        if kind == "W":
            send(src, dst, 0, main, x_send.at[0], dst, across)
            return
        start, width = (0, depth) if step < 4 else (way * half, half)
        send(src, dst, start, width, x_send.at[1 + step // 4], SECOND[dst] if step == 4 and way else dst, across)
        send(place("W", step, way), place("TW", step, way), *strip_of(step, way), x_send.at[3 + step // 4],
             STRIPS["TW", step, way], across)

    def take(kind, step, way):
        piece = place(kind, step, way)
        if kind[-1] == "W":
            start, width = (0, main) if step < 4 else (way * main // 2, main // 2)
        else:
            start, width = (0, depth) if step < 4 else (way * half, half)
        arrived(piece, start, width, SECOND[piece] if step == 4 and way else piece)
        send_sib(piece, start, width, batch_of(piece))
        if kind[-1] == "N":
            wide = kind[:-1] + "W"
            piece = place(wide, step, way)
            arrived(piece, *strip_of(step, way), STRIPS[wide, step, way])
            send_sib(piece, *strip_of(step, way), batch_of(piece) + 3 * (piece == FINAL))

    def sib_batch(b):
        first, count = BATCHES[b]
        count -= b == len(BATCHES) - 1
        here = block.at[first:first + count, 1 - core]
        return remote(here, here, sib_send.at[b], sib_recv.at[b], sibling)

    def sib_last(k):
        here = part(FINAL, 1 - core, k * quarter, quarter)
        sem = len(BATCHES) + k
        return remote(here, here, sib_send.at[sem], sib_recv.at[sem], sibling)

    def take_last(i):
        for k in (2 * i, 2 * i + 1):
            arrived(FINAL, *last_part(k), SECOND[FINAL] + k - 1 if k else FINAL)
            send_sib(FINAL, *last_part(k), len(BATCHES) + i)

    def product(first, count, start, width):
        cols = pl.ds(start if isinstance(start, int) else pl.multiple_of(start, width), width)
        rhs = block[first:first + count, :, :, cols].reshape(count * 32, width)
        return lax.dot_general(grads[:, cols], rhs, (((1,), (1,)), ((), ())), preferred_element_type=jnp.float32)

    def columns(b):
        return b * 256, 256

    def batch(b):
        first, count = BATCHES[b]
        sib_batch(b).wait_recv()
        w = count * 32
        acc[...] = jnp.zeros_like(acc)

        @pl.loop(0, 4)
        def _(k):
            if b == len(BATCHES) - 1:
                sib_last(k).wait_recv()
            acc[:, :w] += product(first, count, k * quarter, quarter)
            if b == len(BATCHES) - 1:
                pl.when(k == 0)(lambda: take_last(3))
        start, width = columns(b)
        tile[:, start:start + w] = acc[:, :w].astype(jnp.bfloat16)

        cols = slice(start, start + width)
        if b >= NEAR_SUMS:
            to = slice(start - NEAR_SUMS * 256, start - NEAR_SUMS * 256 + width)

            @pl.loop(0, GROUP - 1)
            def _(j):
                peer = peer_of(j)
                rows = pl.ds(pl.multiple_of(rows_of(peer) * 64, 64), 64)
                remote(tile.at[rows, cols], inbox.at[j, :, to], red_send.at[b], red_recv.at[b], peer).start()
        else:
            @pl.loop(0, 3)
            def _(j):
                peer = along_y(j)
                rows = pl.ds(pl.multiple_of(lax.rem(peer[1], 4) * 128, 128), 128)
                remote(tile.at[rows, cols], inbox_y.at[j, :, cols], red_send.at[b], red_recv.at[b], peer).start()

    def reduced(b):
        start, width = columns(b)
        late = start - NEAR_SUMS * 256
        here = inbox.at[:, :, late:late + width] if b >= NEAR_SUMS else inbox_y.at[:, :, start:start + width]
        return remote(here, here, red_send.at[b], red_recv.at[b], sibling)

    def swap_x(b):
        start, width = columns(b)
        cols = slice(start, start + width)
        reduced(b).wait_recv()
        total = tile[pl.ds(pl.multiple_of(y * 128, 128), 128), cols].astype(jnp.float32)
        for j in range(3):
            total += inbox_y[j, :, cols].astype(jnp.float32)
        for i in range(2):
            sums[i, :, cols] = total[i * 64:(i + 1) * 64]
            halves[i, :, cols] = total[i * 64:(i + 1) * 64].astype(jnp.bfloat16)
        remote(halves.at[1 - lo, :, cols], inbox_x.at[:, cols], swap_send.at[b], swap_recv.at[0], aside).start()

    def swapped(start, width, b):
        here = inbox_x.at[:, start:start + width]
        return remote(here, here, swap_send.at[b], swap_recv.at[0], sibling)

    pl.semaphore_wait(barrier, 4 + GROUP - 1)
    for way in WAYS:
        round_z("N", 0, way)
    condition(raw.at[16:32], *mats, by_row, by_query, block.at[1, core])
    over_x("W", 0, 0)
    for way in WAYS:
        strip_round_z(0, way)
        round_z("W", 0, way)
    over_x("N", 0, 0)
    loads[4].start()

    loads[3].wait()
    row = lax.broadcasted_iota(jnp.int32, (32, 1), 0)
    row = row + 16 * (row // 16)

    def first_query(piece):
        kind, step, way = PIECES[piece]
        zz = lax.rem(z + (Z - step if way == FWD else step), Z)
        hh = 1 - hi if kind[0] == "T" else hi
        return (hh * Z + zz) * 64 + (16 if kind[-1] == "W" else 0)

    for piece in range(len(PIECES)):
        rows = slice(piece * 32, (piece + 1) * 32)
        pick[rows, :] = jnp.where(row + first_query(piece) == order[...], 1.0, 0.0).astype(jnp.bfloat16)
    def ordered(total, start):
        high = total.astype(jnp.bfloat16)
        low = (total - high.astype(jnp.float32)).astype(jnp.bfloat16)
        both = jnp.dot(jnp.concatenate([high, low], axis=0), pick[start:start + total.shape[1], :],
                       preferred_element_type=jnp.float32)
        return both[:64] + both[64:]

    def late_sum(b):
        start, width = columns(b)
        reduced(b).wait_recv()
        total = tile[pl.ds(pl.multiple_of(rows_of((ex, me)) * 64, 64), 64), start:start + width].astype(jnp.float32)
        for j in range(GROUP - 1):
            total += inbox[j, :, start - NEAR_SUMS * 256:start - NEAR_SUMS * 256 + width].astype(jnp.float32)
        return ordered(total, start)

    for way in WAYS:
        take("N", 1, way)
        round_z("N", 1, way)
    for way in WAYS:
        over_x("N", 1, way)
    for piece in (0, 1):
        send_sib(piece, 0, depth, 0)
    take("TW", 0, 0)
    for way in WAYS:
        round_z("TW", 0, way)
    for way in WAYS:
        take("W", 1, way)
    take("TN", 0, 0)
    loads[4].wait()
    batch(0)
    for way in WAYS:
        take("N", 2, way)
        round_z("N", 2, way)
        over_x("N", 2, way)
    for way in WAYS:
        round_z("W", 1, way)
    for kind in ("TW", "TN"):
        for way in WAYS:
            take(kind, 1, way)
    for way in WAYS:
        take("N", 3, way)
        round_z("N", 3, way)
        over_x("N", 3, way)
    for way in WAYS:
        round_z("TW", 1, way)
    batch(1)
    for way in WAYS:
        take("W", 2, way)
        round_z("W", 2, way)
    for way in WAYS:
        take("N", 4, way)
        over_x("N", 4, way)
    for way in WAYS:
        take("TN", 2, way)
    for way in WAYS:
        take("TW", 2, way)
        round_z("TW", 2, way)
    for way in WAYS:
        take("W", 3, way)
        round_z("W", 3, way)
    swap_x(0)
    swap_x(1)
    batch(2)
    for way in WAYS:
        take("TN", 3, way)
    for way in WAYS:
        take("TW", 3, way)
        round_z("TW", 3, way)
    for kind in ("W", "TN"):
        for way in WAYS:
            take(kind, 4, way)
    for i in range(3):
        take_last(i)
    swap_x(2)
    batch(3)
    swapped(0, NEAR_SUMS * 256, 0).wait_recv()
    scores[...] = ordered(sums[lo] + inbox_x[...].astype(jnp.float32), 0)
    done = (scores[...] + late_sum(3)).astype(jnp.bfloat16)
    for m in range(GROUP):
        outbox[m] = done[:, m * 128:(m + 1) * 128]

    @pl.loop(0, GROUP - 1)
    def _(j):
        peer = peer_of(j)
        remote(outbox.at[peer[1]], final.at[rows_of((ex, me))], fin_send.at[0], fin_recv.at[0], peer).start()
    final[rows_of((ex, me))] = outbox[me]

    def units(n, width, sem):
        here = block.at[0:n, core, :, 0:width]
        remote(here, here, sem, main_recv.at[0], sibling).wait_send()

    for step in range(4):
        parts = 1 if step < 3 else 2
        units(2, depth // parts, z_send.at[step])
        units(4, main // parts, z_send.at[4 + step])
        units(2, STRIP // parts, z_send.at[8 + step])
    for sem, (n, width) in enumerate(((1, main), (7, depth), (2, half), (7, STRIP), (2, STRIP // 2))):
        units(n, width, x_send.at[sem])
    for b in range(len(BATCHES)):
        sib_batch(b).wait_send()
        reduced(b).wait_send()
    for b in range(NEAR_SUMS):
        swapped(0, 256, b).wait_send()
    for k in range(4):
        sib_last(k).wait_send()
    whole = remote(final.at[0:GROUP - 1], final.at[0:GROUP - 1], fin_send.at[0], fin_recv.at[0], sibling)
    whole.wait_send()
    whole.wait_recv()
    out_ref[...] = final[...].reshape(out_ref.shape).astype(jnp.float32) * (1.0 / 256.0)


def local(train_grads, query_grads, left_factor, right_factor, query_order):
    grads = train_grads[:, 0, :]
    raw = query_grads[:, 0, :]
    rows, depth = grads.shape
    own = raw.shape[0]
    queries = query_order.shape[0]
    dma = pltpu.SemaphoreType.DMA
    return pl.pallas_call(
        kernel,
        name="scores",
        out_shape=jax.ShapeDtypeStruct((rows, queries // GROUP), jnp.float32),
        in_specs=[pl.BlockSpec(memory_space=pl.ANY)] * 5,
        out_specs=pl.BlockSpec(memory_space=pltpu.VMEM),
        scratch_shapes=[
            pltpu.VMEM((own, depth), jnp.bfloat16),
            pltpu.VMEM((FA, FA), jnp.float32),
            pltpu.VMEM((FB, FB), jnp.float32),
            pltpu.VMEM((1, queries), jnp.int32),
            pltpu.VMEM((own * FA, FB), jnp.float32),
            pltpu.VMEM((own * FA, FB), jnp.float32),
            pltpu.VMEM((rows, depth), jnp.bfloat16),
            pltpu.VMEM((len(PIECES), 2, own // 2, depth), jnp.bfloat16),
            pltpu.VMEM((rows, 256), jnp.float32),
            pltpu.VMEM((rows, COLUMNS), jnp.bfloat16),
            pltpu.VMEM((COLUMNS, queries), jnp.bfloat16),
            pltpu.VMEM((rows // GROUP, queries), jnp.float32),
            pltpu.VMEM((2, rows // GROUP, NEAR_SUMS * 256), jnp.float32),
            pltpu.VMEM((2, rows // GROUP, NEAR_SUMS * 256), jnp.bfloat16),
            pltpu.VMEM((GROUP - 1, rows // GROUP, COLUMNS - NEAR_SUMS * 256), jnp.bfloat16),
            pltpu.VMEM((3, rows // 4, NEAR_SUMS * 256), jnp.bfloat16),
            pltpu.VMEM((rows // GROUP, NEAR_SUMS * 256), jnp.bfloat16),
            pltpu.VMEM((GROUP, rows // GROUP, queries // GROUP), jnp.bfloat16),
            pltpu.VMEM((GROUP, rows // GROUP, queries // GROUP), jnp.bfloat16),
            dma((5,)),
            dma((ARRIVALS,)),
            dma((12,)),
            dma((5,)),
            dma((len(BATCHES) + 4,)),
            dma((len(BATCHES) + 4,)),
            dma((len(BATCHES),)),
            dma((len(BATCHES),)),
            dma((NEAR_SUMS,)),
            dma((1,)),
            dma((1,)),
            dma((1,)),
        ],
        compiler_params=pltpu.CompilerParams(
            collective_id=0, has_side_effects=True, vmem_limit_bytes=52 * 2**20
        ),
        cost_estimate=pl.CostEstimate(
            flops=2 * rows * depth * queries, bytes_accessed=rows * depth * 2, transcendentals=0
        ),
    )(*(pltpu.with_memory_space_constraint(x, pltpu.HBM) for x in (
        raw, grads, left_factor[0], right_factor[0], query_order.reshape(1, queries))))


def solution(mesh):
    return jax.shard_map(
        local,
        mesh=mesh,
        in_specs=(
            P("ex", "layer", None),
            P("ex", "layer", None),
            P("layer", None, None),
            P("layer", None, None),
            P(),
        ),
        out_specs=P("ex", "layer"),
        check_vma=False,
    )
```
